256 devices in a mesh: mp: 4 (over z_lo), seq: 32 (over x, z_hi, y), tp: 2 (over core).
Axes of the slice: x: 4, y: 4, z: 8 (z_hi: 2, z_lo: 4; z = z_hi * 4 + z_lo), core: 2. Of those that a mesh axis runs over, the one named last changes fastest.
Arguments:
- latent_noise: bfloat16 [2048, 64], P(('mp', 'tp')), may hold values from -6 to 6
- score_noise: bfloat16 [2048, 64], P(('mp', 'tp')), may hold values from -6 to 6
- gen_step: int32 [1], replicated, may hold values from 600 to 999
- score_step: int32 [1], replicated, may hold values from 100 to 949
- embed_weight: bfloat16 [4, 64, 5120], P('mp'), may hold values from -0.75 to 0.75
- qkv_weight: bfloat16 [4, 32, 384, 5120], P('mp', 'seq'), may hold values from -0.078125 to 0.078125
- mod_weight: bfloat16 [4, 256, 10240], P('mp'), may hold values from -0.375 to 0.375
- head_out: bfloat16 [4, 32, 128, 64], P('mp', 'seq'), may hold values from -0.09375 to 0.09375
Outputs:
- generated: bfloat16 [2048, 64], P(('mp', 'tp'))
- dmd_grad: float32 [2048, 64], P(('mp', 'tp'))
The draws below stay inside these ranges and needn't reach their ends.
All inputs are finite; a program needn't handle non-finite values.
Results may differ from the reference program's by a relative error of at most 0.014.
Values may be sent and summed in bfloat16 or wider, within the bound.
No kernel may reach another device: no remote copies, remote signals or barrier semaphores. Data moves between devices by JAX's collectives and lax.ppermute only.
A program may use at most 128 MiB of HBM per device.

```python
import math
import jax
import jax.numpy as jnp
from jax import lax

D = 5120
H = 32
DH = 128
C = 64
FREQ = 256
TOKENS = 2048


def shard_levels(key, shape, cuts, low, largest):
    gain = 1.0
    for axis_at, shards_of in cuts:
        heights = jax.random.uniform(jax.random.fold_in(jax.random.fold_in(key, 6), axis_at), (shards_of,), jnp.float32, low / len(cuts), largest / len(cuts))
        gain = gain * jnp.repeat(jnp.exp(heights), shape[axis_at] // shards_of).reshape((-1,) + (1,) * (len(shape) - 1 - axis_at))
    return gain


def bell_draw(stream_key, shape, scale, reach, shards=(), held_as=jnp.bfloat16):
    drawn = scale * jax.random.normal(stream_key, shape, jnp.float32)
    if shards:
        drawn = drawn * shard_levels(stream_key, shape, shards, -0.22, 0.18)
    return jnp.clip(drawn, -reach, reach).astype(held_as)


def setup_inputs(seed: int = 0) -> dict:
    arg_keys = jax.random.split(jax.random.key(seed), 9)
    latent_noise = bell_draw(arg_keys[0], (TOKENS, C), 1.0, 6.0, ((0, 8),))
    score_noise = bell_draw(arg_keys[1], (TOKENS, C), 1.0, 6.0, ((0, 8),))
    gen_step = jax.random.randint(arg_keys[2], (1,), 600, 1000).astype(jnp.int32)
    score_step = jax.random.randint(arg_keys[3], (1,), 100, 950).astype(jnp.int32)
    embed_weight = bell_draw(arg_keys[4], (4, C, D), C ** -0.5, 0.75, ((0, 4),))
    qkv_weight = bell_draw(arg_keys[5], (4, H, 3 * DH, D), D ** -0.5, 0.078125, ((0, 4), (1, 32)))
    mod_weight = bell_draw(arg_keys[6], (4, FREQ, 2 * D), FREQ ** -0.5, 0.375, ((0, 4),))
    head_out = bell_draw(arg_keys[7], (4, H, DH, C), (H * DH) ** -0.5, 0.09375, ((0, 4), (1, 32)))
    return dict(latent_noise=latent_noise, score_noise=score_noise, gen_step=gen_step, score_step=score_step, embed_weight=embed_weight, qkv_weight=qkv_weight, mod_weight=mod_weight, head_out=head_out)


norm_eps = 1e-06
guide_weight = 2.0
step_scale = 1000.0

def sinusoid(step_index):
    half_freq = FREQ // 2
    frequency = jnp.exp(-math.log(10000.0) * jnp.arange(half_freq, dtype=jnp.float32) * 2.0 / FREQ)
    angles = step_index.astype(jnp.float32)[0] * frequency
    return jnp.concatenate([jnp.cos(angles), jnp.sin(angles)])

def modulation(step_index, weight):
    return jnp.dot(sinusoid(step_index)[None, :], weight.astype(jnp.float32), precision=lax.Precision.HIGHEST)[0]

def run_model(latent, embed_w, qkv_w, head_w, mod_vec):
    embedded = jnp.dot(latent, embed_w, preferred_element_type=jnp.float32)
    row_mean = lax.optimization_barrier(jnp.mean(embedded, -1, keepdims=True))
    row_var = lax.optimization_barrier(jnp.mean(embedded * embedded, -1, keepdims=True)) - row_mean * row_mean
    normed = ((embedded - row_mean) * lax.rsqrt(row_var + norm_eps) * (1.0 + mod_vec[D:]) + mod_vec[:D]).astype(jnp.bfloat16)

    def one_head(head_args):
        weight, out_map = head_args
        projected = lax.dot_general(normed, weight, (((1,), (1,)), ((), ())), preferred_element_type=jnp.float32).astype(jnp.bfloat16)
        queries = projected[:, :DH]
        key_rows = projected[:, DH:2 * DH]
        value_rows = projected[:, 2 * DH:]
        logits = jnp.dot(queries, key_rows.T, preferred_element_type=jnp.float32) * DH ** (-0.5)
        logits = logits - lax.optimization_barrier(jnp.max(logits, -1, keepdims=True))
        expo = jnp.exp(logits)
        attn_probs = (expo / lax.optimization_barrier(jnp.sum(expo, -1, keepdims=True))).astype(jnp.bfloat16)
        attended = jnp.dot(attn_probs, value_rows, preferred_element_type=jnp.float32).astype(jnp.bfloat16)
        return jnp.dot(attended, out_map, preferred_element_type=jnp.float32)
    head_terms = lax.map(one_head, (qkv_w, head_w))
    return lax.optimization_barrier(jnp.sum(head_terms, 0))

def reference(latent_noise, score_noise, gen_step, score_step, embed_weight, qkv_weight, mod_weight, head_out):
    gen_sigma = gen_step[0].astype(jnp.float32) / step_scale
    score_sigma = score_step[0].astype(jnp.float32) / step_scale
    velocity = run_model(latent_noise, embed_weight[0], qkv_weight[0], head_out[0], modulation(gen_step, mod_weight[0]))
    clean = latent_noise.astype(jnp.float32) - gen_sigma * velocity
    noisy_latent = ((1.0 - score_sigma) * clean + score_sigma * score_noise.astype(jnp.float32)).astype(jnp.bfloat16)
    predicted = []
    for model_index in range(1, 4):
        velocity = run_model(noisy_latent, embed_weight[model_index], qkv_weight[model_index], head_out[model_index], modulation(score_step, mod_weight[model_index]))
        predicted.append(noisy_latent.astype(jnp.float32) - score_sigma * velocity)
    real_guided = predicted[2] + guide_weight * (predicted[1] - predicted[2])
    dmd_grad = predicted[0] - real_guided
    return (clean.astype(jnp.bfloat16), dmd_grad)
```

```python
import functools
import math

import jax
import jax.numpy as jnp
from jax import lax
from jax.experimental import pallas as pl
from jax.experimental.pallas import tpu as pltpu
from jax.sharding import Mesh
from jax.sharding import PartitionSpec as P

norm_eps = 1e-06
step_scale = 1000.0
f32 = jnp.float32
bf16 = jnp.bfloat16
chunk = 1024
lanes = 128
part = 80


def frequencies(freq_count):
    half_freq = freq_count // 2
    index = lax.broadcasted_iota(jnp.int32, (1, half_freq), 1)
    total = jnp.ones((1, half_freq), f32)
    for bit in range(half_freq.bit_length() - 1):
        factor = 10000.0 ** (-2.0 * (1 << bit) / freq_count)
        total = total * jnp.where((index >> bit) & 1 == 1, factor, 1.0)
    return total


def cos_sin(angle):
    turn = jnp.floor(angle * (2.0 / math.pi) + 0.5)
    left = angle - turn * 1.5703125
    left = left - turn * 4.837512969970703125e-4
    left = left - turn * 7.54978995489188216e-8
    square = left * left
    sine = left + left * square * (
        -1.6666654611e-1 + square * (8.3321608736e-3 - square * 1.9515295891e-4)
    )
    cosine = (
        1.0
        - 0.5 * square
        + square
        * square
        * (4.166664568298827e-2 + square * (-1.388731625493765e-3 + square * 2.443315711809948e-5))
    )
    quarter = turn.astype(jnp.int32) & 3
    odd = (quarter & 1) == 1
    cos_out = jnp.where(odd, sine, cosine)
    sin_out = jnp.where(odd, cosine, sine)
    cos_out = jnp.where((quarter == 1) | (quarter == 2), -cos_out, cos_out)
    sin_out = jnp.where(quarter >= 2, -sin_out, sin_out)
    return cos_out, sin_out


def dot(a, b, dims=(1, 0), precision=None):
    return lax.dot_general(
        a, b, (((dims[0],), (dims[1],)), ((), ())), precision=precision, preferred_element_type=f32
    )


def halves(value):
    high = value.astype(bf16)
    return high, (value - high.astype(f32)).astype(bf16)


def dot_halves(a, b):
    a_high, a_low = halves(a)
    b_high, b_low = halves(b)
    return dot(
        jnp.concatenate([a_high, a_high, a_low], 0),
        jnp.concatenate([b_high, b_low, b_high], 0),
        (0, 0),
    )


def maps_kernel(
    gen_ref, score_ref, embed_hbm, head_hbm, mod_hbm, weight_hbm, out_ref,
    embed_ref, head_ref, mod_ref, weight_ref, sems,
):
    chans, head_size = head_ref.shape
    width = embed_ref.shape[1]
    steps = width // chunk
    small = [
        pltpu.make_async_copy(source, target, sems.at[at])
        for at, (source, target) in enumerate(
            ((embed_hbm, embed_ref), (head_hbm, head_ref))
        )
    ]
    for copy in small:
        copy.start()
    copies = []
    for step in range(steps):
        mine = []
        for kind, (source, target, offset) in enumerate(
            ((mod_hbm, mod_ref, 0), (mod_hbm, mod_ref, width), (weight_hbm, weight_ref, 0))
        ):
            at = pl.ds(offset + step * chunk, chunk)
            copy = pltpu.make_async_copy(
                source.at[:, at], target.at[:, at], sems.at[2 + 3 * step + kind]
            )
            copy.start()
            mine.append(copy)
        copies.append(mine)

    small[0].wait()
    mean = jnp.sum(embed_ref[...].astype(f32), 1, keepdims=True) * (1.0 / width)
    ones = jnp.ones((part - chans, chunk), bf16)
    row_at = lax.broadcasted_iota(jnp.int32, (lanes - chans, chunk), 0)
    own_step = jnp.where(lax.axis_index("mp") == 0, gen_ref[0], score_ref[0]).astype(f32)
    waves = cos_sin(frequencies(2 * lanes) * own_step)
    freq = jnp.concatenate([jnp.broadcast_to(wave, (lanes, lanes)).T for wave in waves], 0)
    maps = gram = None
    for step in range(steps):
        own = embed_ref[:, pl.ds(step * chunk, chunk)]
        gram_term = dot(jnp.concatenate([own, ones], 0), own, (1, 1))
        rows = []
        copies[step][0].wait()
        copies[step][1].wait()
        for kind in range(2):
            total = None
            for at in range(0, freq.shape[0], 16):
                here = mod_ref[at : at + 16, pl.ds(kind * width + step * chunk, chunk)]
                scale = jnp.concatenate([freq[at : at + 16]] * (chunk // lanes), 1)
                term = here.astype(f32) * scale
                total = term if total is None else total + term
            rows.append(jnp.sum(total, 0, keepdims=True))
        centred = (own.astype(f32) - mean) * (1.0 + rows[1])
        tail = jnp.where(row_at == 0, jnp.broadcast_to(rows[0], row_at.shape), 0.0)
        lifted = jnp.concatenate([centred.astype(bf16), tail.astype(bf16)], 0)
        copies[step][2].wait()
        maps_term = dot(weight_ref[:, pl.ds(step * chunk, chunk)], lifted, (1, 1))
        maps = maps_term if maps is None else maps + maps_term
        gram = gram_term if gram is None else gram + gram_term

    map_q = maps[:head_size] * (head_size ** (-0.5) * math.log2(math.e))
    map_k = maps[head_size : 2 * head_size]
    map_v = maps[2 * head_size :]
    lane = lax.broadcasted_iota(jnp.int32, (head_size, lanes), 1)
    small[1].wait()
    wide_head = jnp.concatenate([jnp.zeros_like(head_ref), head_ref[...]], 0)
    main = dot_halves(map_q, jnp.where(lane < chans, map_k, 0.0))
    high, low = halves(map_v)
    main += dot(high, wide_head, (0, 1)) + dot(low, wide_head, (0, 1))
    last = dot_halves(map_k, map_q)[chans : chans + 1]
    main = main[:part]
    row = lax.broadcasted_iota(jnp.int32, main.shape, 0)
    main = jnp.where(row == chans + 1, jnp.broadcast_to(last, main.shape), main)
    out_ref[:part] = main.astype(bf16)
    gram = gram * (1.0 / width)
    high, low = halves(gram[:chans] - mean * gram[chans : chans + 1])
    out_ref[part:] = jnp.concatenate([high.astype(f32), low.astype(f32)], 1).astype(bf16)


def fold_maps(gen_step, score_step, head, embed, mod_weight, weight):
    chans, width = embed.shape
    return pl.pallas_call(
        maps_kernel,
        in_specs=[pl.BlockSpec(memory_space=pltpu.SMEM)] * 2
        + [pl.BlockSpec(memory_space=pl.ANY)] * 4,
        out_specs=pl.BlockSpec(memory_space=pltpu.VMEM),
        out_shape=jax.ShapeDtypeStruct((part + chans, lanes), bf16),
        scratch_shapes=[
            pltpu.VMEM(embed.shape, bf16),
            pltpu.VMEM(head.shape, bf16),
            pltpu.VMEM(mod_weight.shape, bf16),
            pltpu.VMEM(weight.shape, bf16),
            pltpu.SemaphoreType.DMA((2 + 3 * (width // chunk),)),
        ],
        compiler_params=pltpu.CompilerParams(vmem_limit_bytes=56_000_000),
        cost_estimate=pl.CostEstimate(
            flops=6_000_000_000, bytes_accessed=10_000_000, transcendentals=0
        ),
        name="fold_maps",
    )(gen_step, score_step, embed, head, mod_weight, weight)


def attend_kernel(terms, count, before, last, *refs):
    refs = list(refs)
    pack_refs, own_ref, token_refs = refs[:4], refs[4], refs[5 : 5 + count]
    keys_ref = refs[-1]
    chans, rows = own_ref.shape
    size = count * rows
    here, upper = lax.axis_index("mp"), lax.axis_index("zh") == 1

    mains, spreads = [], []
    for model, _ in terms:
        at = here ^ model
        pack = pack_refs[0][...]
        for other in range(1, 4):
            pack = jnp.where(at == other, pack_refs[other][...], pack)
        one, two = pack[:part], pack[part + chans :]
        mains.append((jnp.where(upper, two, one), jnp.where(upper, one, two)))
        spreads.append(pack[part : part + chans])

    tokens = jnp.concatenate([ref[...] for ref in token_refs] + [own_ref[...]], 1)
    wide = tokens.astype(f32)
    spread = dot(jnp.concatenate(spreads, 0), jnp.concatenate([tokens, tokens], 0))
    row = lax.broadcasted_iota(jnp.int32, (part - chans, size + rows), 0)
    one = jnp.where(row == 0, 1.0, 0.0).astype(bf16)
    logits = []
    for slot, heads in enumerate(mains):
        product = spread[slot * chans : (slot + 1) * chans] * wide
        variance = jnp.maximum(jnp.sum(product, 0, keepdims=True), 0.0)
        normed = wide * lax.rsqrt(variance + norm_eps)
        high = normed.astype(bf16)
        low = (normed - high.astype(f32)).astype(bf16)
        features = jnp.concatenate([high, one, low, jnp.zeros_like(one)], 0)
        keys_ref[slot] = features[:, :size]
        own = features[:, size:]
        own_high = jnp.concatenate([own[:part], jnp.zeros((lanes - part, rows), bf16)], 0)
        for main in heads:
            ask = dot(jnp.concatenate([main, main], 0), own, (0, 0))[:chans].astype(bf16)
            shared = jnp.broadcast_to(dot(main[chans:], own_high)[1:2], (part - chans, rows))
            shared = jnp.where(row[:, :rows] == 0, shared, 0.0).astype(bf16)
            queries = jnp.concatenate([ask, shared, ask, jnp.zeros_like(shared)], 0)
            logits.append(dot(queries, keys_ref[slot], (0, 0)))

    total = None
    for place, scores in enumerate(logits):
        slot, head = divmod(place, 2)
        peak = jnp.broadcast_to(jnp.max(scores, 1, keepdims=True), (rows, lanes))
        if before:
            old_peak = refs[6 + count][place]
            peak = jnp.maximum(peak, old_peak)
        expo = jnp.exp2(scores - jnp.concatenate([peak] * (size // lanes), 1)).astype(bf16)
        mixed = dot(expo, keys_ref[slot], (1, 1))
        if before:
            factor = jnp.exp2(old_peak - peak)
            factor = jnp.concatenate([factor, factor[:, : 2 * part - lanes]], 1)
            mixed += refs[5 + count][place] * factor
        if last:
            mixed = (mixed / mixed[:, chans : chans + 1]).astype(bf16)
            main = jnp.concatenate([mains[slot][head]] * 2, 0)
            term = terms[slot][1] * dot(main, mixed, (0, 1))[chans:]
            total = term if total is None else total + term
        else:
            refs[-3][place] = mixed
            refs[-2][place] = peak
    if last:
        refs[-2][...] = total.astype(bf16)


def attend(terms, packs, own, tokens, state=(), last=True):
    rows = own.shape[1]
    count = len(tokens)
    pairs = 2 * count * rows * rows * len(terms)
    shape = [
        jax.ShapeDtypeStruct((2 * len(terms), rows, 2 * part), f32),
        jax.ShapeDtypeStruct((2 * len(terms), rows, lanes), f32),
    ]
    if last:
        shape = jax.ShapeDtypeStruct(own.shape, bf16)
    return pl.pallas_call(
        functools.partial(attend_kernel, terms, count, bool(state), last),
        out_shape=shape,
        scratch_shapes=[pltpu.VMEM((len(terms), 2 * part, count * rows), bf16)],
        compiler_params=pltpu.CompilerParams(vmem_limit_bytes=48 * 1024 * 1024),
        cost_estimate=pl.CostEstimate(
            flops=16 * pairs * lanes, bytes_accessed=1_000_000, transcendentals=pairs
        ),
        name="attend",
    )(*packs, own, *tokens, *state)


def swap(value, axis, flip, cross=0):
    axes = (axis, "tp")
    flip = 2 * flip + cross
    return lax.ppermute(value, axes, [(i, i ^ flip) for i in range(lax.axis_size(axes))])


def swap_all(value, axis, cross):
    one, three, two = (
        swap(value, axis, flip, crossed)
        for flip, crossed in ((1, cross[0]), (3, cross[2]), (2, cross[1]))
    )
    return [value, one, two, three]


def other_core(value):
    return lax.ppermute(value, "tp", [(0, 1), (1, 0)])


def add_over(value, axis):
    sent = lax.optimization_barrier(value.astype(bf16))
    parts = [part.astype(f32) for part in swap_all(sent, axis, (1, 0, 1))]
    return (parts[0] + parts[1]) + (parts[2] + parts[3])


def add_heads(value):
    return add_over(add_over(value, "y"), "x")


def shards(
    latent_noise, score_noise, gen_step, score_step, embed_weight, qkv_weight, mod_weight, head_out
):
    model = lax.axis_index("mp")
    gen_sigma = gen_step[0].astype(f32) / step_scale
    score_sigma = score_step[0].astype(f32) / step_scale
    latents, noise = latent_noise.T, score_noise.T
    odd = (lax.axis_index("x") + lax.axis_index("y")) % 2 == 1

    first = swap(latents, "mp", 1, 1)
    noise = jnp.where(odd, other_core(noise), noise)
    pack = fold_maps(
        gen_step, score_step, head_out[0, 0].T, embed_weight[0], mod_weight[0], qkv_weight[0, 0]
    )
    pack, first, noise = lax.optimization_barrier((pack, first, noise))
    other = swap(pack[:part], "zh", 1, 1)
    pair = swap(jnp.stack([latents, first]), "mp", 2, 1)
    packs = swap_all(jnp.concatenate([pack, other], 0), "mp", (1, 1, 1))
    near = [latents, first, pair[0], pair[1]]
    far = other_core(jnp.stack(near))

    latents = jnp.where(odd, far[0], latents)
    speed = add_heads(attend(((0, 1.0),), packs, latents, near + list(far)))
    clean = latents.astype(f32) - gen_sigma * speed
    noisy = (1.0 - score_sigma) * clean + score_sigma * noise.astype(f32)
    near = swap_all(noisy.astype(bf16), "mp", (1, 1, 1))
    far = other_core(jnp.stack(near))
    terms = ((1, 1.0), (2, -2.0), (3, 1.0))
    state = attend(terms, packs, near[0], near, last=False)
    grad = attend(terms, packs, near[0], list(far), state)
    grad = add_heads(grad) * -score_sigma
    grad = jnp.where(odd, other_core(grad), grad)
    clean = clean.astype(bf16)
    clean = jnp.where(odd, other_core(clean), clean)
    return (clean.T, grad.T)


def solution(mesh):
    models, heads, cores = mesh.devices.shape
    fine = Mesh(mesh.devices.reshape(models, 4, heads // 16, 4, cores), ("mp", "x", "zh", "y", "tp"))
    placed = (
        P(("mp", "tp"), None),
        P(("mp", "tp"), None),
        P(),
        P(),
        P("mp", None, None),
        P("mp", ("x", "zh", "y"), None, None),
        P("mp", None, None),
        P("mp", ("x", "zh", "y"), None, None),
    )
    return jax.shard_map(
        shards,
        mesh=fine,
        in_specs=placed,
        out_specs=(P(("mp", "tp"), None), P(("mp", "tp"), None)),
        check_vma=False,
    )
```

```python
import functools
import math

import jax
import jax.numpy as jnp
from jax import lax
from jax.experimental import pallas as pl
from jax.experimental.pallas import tpu as pltpu
from jax.sharding import Mesh
from jax.sharding import PartitionSpec as P

norm_eps = 1e-06
step_scale = 1000.0
f32 = jnp.float32
bf16 = jnp.bfloat16
chunk = 1024
lanes = 128
part = 80


def frequencies(freq_count):
    half_freq = freq_count // 2
    index = lax.broadcasted_iota(jnp.int32, (1, half_freq), 1)
    total = jnp.ones((1, half_freq), f32)
    for bit in range(half_freq.bit_length() - 1):
        factor = 10000.0 ** (-2.0 * (1 << bit) / freq_count)
        total = total * jnp.where((index >> bit) & 1 == 1, factor, 1.0)
    return total


def cos_sin(angle):
    turn = jnp.floor(angle * (2.0 / math.pi) + 0.5)
    left = angle - turn * 1.5703125
    left = left - turn * 4.837512969970703125e-4
    left = left - turn * 7.54978995489188216e-8
    square = left * left
    sine = left + left * square * (
        -1.6666654611e-1 + square * (8.3321608736e-3 - square * 1.9515295891e-4)
    )
    cosine = (
        1.0
        - 0.5 * square
        + square
        * square
        * (4.166664568298827e-2 + square * (-1.388731625493765e-3 + square * 2.443315711809948e-5))
    )
    quarter = turn.astype(jnp.int32) & 3
    odd = (quarter & 1) == 1
    cos_out = jnp.where(odd, sine, cosine)
    sin_out = jnp.where(odd, cosine, sine)
    cos_out = jnp.where((quarter == 1) | (quarter == 2), -cos_out, cos_out)
    sin_out = jnp.where(quarter >= 2, -sin_out, sin_out)
    return cos_out, sin_out


def dot(a, b, dims=(1, 0), precision=None):
    return lax.dot_general(
        a, b, (((dims[0],), (dims[1],)), ((), ())), precision=precision, preferred_element_type=f32
    )


def halves(value):
    high = value.astype(bf16)
    return high, (value - high.astype(f32)).astype(bf16)


def dot_halves(a, b):
    a_high, a_low = halves(a)
    b_high, b_low = halves(b)
    return dot(
        jnp.concatenate([a_high, a_high, a_low], 0),
        jnp.concatenate([b_high, b_low, b_high], 0),
        (0, 0),
    )


def maps_kernel(
    gen_ref, score_ref, embed_hbm, head_hbm, mod_hbm, weight_hbm, out_ref,
    embed_ref, head_ref, mod_ref, weight_ref, sems,
):
    chans, head_size = head_ref.shape
    width = embed_ref.shape[1]
    steps = width // chunk
    small = [
        pltpu.make_async_copy(source, target, sems.at[at])
        for at, (source, target) in enumerate(
            ((embed_hbm, embed_ref), (head_hbm, head_ref))
        )
    ]
    for copy in small:
        copy.start()
    copies = []
    for step in range(steps):
        mine = []
        for kind, (source, target, offset) in enumerate(
            ((mod_hbm, mod_ref, 0), (mod_hbm, mod_ref, width), (weight_hbm, weight_ref, 0))
        ):
            at = pl.ds(offset + step * chunk, chunk)
            copy = pltpu.make_async_copy(
                source.at[:, at], target.at[:, at], sems.at[2 + 3 * step + kind]
            )
            copy.start()
            mine.append(copy)
        copies.append(mine)

    small[0].wait()
    mean = jnp.sum(embed_ref[...].astype(f32), 1, keepdims=True) * (1.0 / width)
    ones = jnp.ones((part - chans, chunk), bf16)
    row_at = lax.broadcasted_iota(jnp.int32, (lanes - chans, chunk), 0)
    own_step = jnp.where(lax.axis_index("mp") == 0, gen_ref[0], score_ref[0]).astype(f32)
    waves = cos_sin(frequencies(2 * lanes) * own_step)
    freq = jnp.concatenate([jnp.broadcast_to(wave, (lanes, lanes)).T for wave in waves], 0)
    maps = gram = None
    for step in range(steps):
        own = embed_ref[:, pl.ds(step * chunk, chunk)]
        gram_term = dot(jnp.concatenate([own, ones], 0), own, (1, 1))
        rows = []
        copies[step][0].wait()
        copies[step][1].wait()
        for kind in range(2):
            total = None
            for at in range(0, freq.shape[0], 16):
                here = mod_ref[at : at + 16, pl.ds(kind * width + step * chunk, chunk)]
                scale = jnp.concatenate([freq[at : at + 16]] * (chunk // lanes), 1)
                term = here.astype(f32) * scale
                total = term if total is None else total + term
            rows.append(jnp.sum(total, 0, keepdims=True))
        centred = (own.astype(f32) - mean) * (1.0 + rows[1])
        tail = jnp.where(row_at == 0, jnp.broadcast_to(rows[0], row_at.shape), 0.0)
        lifted = jnp.concatenate([centred.astype(bf16), tail.astype(bf16)], 0)
        copies[step][2].wait()
        maps_term = dot(weight_ref[:, pl.ds(step * chunk, chunk)], lifted, (1, 1))
        maps = maps_term if maps is None else maps + maps_term
        gram = gram_term if gram is None else gram + gram_term

    map_q = maps[:head_size] * (head_size ** (-0.5) * math.log2(math.e))
    map_k = maps[head_size : 2 * head_size]
    map_v = maps[2 * head_size :]
    lane = lax.broadcasted_iota(jnp.int32, (head_size, lanes), 1)
    small[1].wait()
    wide_head = jnp.concatenate([jnp.zeros_like(head_ref), head_ref[...]], 0)
    main = dot_halves(map_q, jnp.where(lane < chans, map_k, 0.0))
    high, low = halves(map_v)
    main += dot(high, wide_head, (0, 1)) + dot(low, wide_head, (0, 1))
    last = dot_halves(map_k, map_q)[chans : chans + 1]
    main = main[:part]
    row = lax.broadcasted_iota(jnp.int32, main.shape, 0)
    main = jnp.where(row == chans + 1, jnp.broadcast_to(last, main.shape), main)
    out_ref[:part] = main.astype(bf16)
    gram = gram * (1.0 / width)
    high, low = halves(gram[:chans] - mean * gram[chans : chans + 1])
    out_ref[part:] = jnp.concatenate([high.astype(f32), low.astype(f32)], 1).astype(bf16)


def fold_maps(gen_step, score_step, head, embed, mod_weight, weight):
    chans, width = embed.shape
    return pl.pallas_call(
        maps_kernel,
        in_specs=[pl.BlockSpec(memory_space=pltpu.SMEM)] * 2
        + [pl.BlockSpec(memory_space=pl.ANY)] * 4,
        out_specs=pl.BlockSpec(memory_space=pltpu.VMEM),
        out_shape=jax.ShapeDtypeStruct((part + chans, lanes), bf16),
        scratch_shapes=[
            pltpu.VMEM(embed.shape, bf16),
            pltpu.VMEM(head.shape, bf16),
            pltpu.VMEM(mod_weight.shape, bf16),
            pltpu.VMEM(weight.shape, bf16),
            pltpu.SemaphoreType.DMA((2 + 3 * (width // chunk),)),
        ],
        compiler_params=pltpu.CompilerParams(vmem_limit_bytes=56_000_000),
        cost_estimate=pl.CostEstimate(
            flops=6_000_000_000, bytes_accessed=10_000_000, transcendentals=0
        ),
        name="fold_maps",
    )(gen_step, score_step, embed, head, mod_weight, weight)


def attend_kernel(terms, count, before, last, *refs):
    refs = list(refs)
    pack_refs, own_ref, token_refs = refs[:4], refs[4], refs[5 : 5 + count]
    keys_ref = refs[-1]
    chans, rows = own_ref.shape
    size = count * rows
    here, upper = lax.axis_index("mp"), lax.axis_index("zh") == 1

    mains, spreads = [], []
    for model, _ in terms:
        at = here ^ model
        pack = pack_refs[0][...]
        for other in range(1, 4):
            pack = jnp.where(at == other, pack_refs[other][...], pack)
        one, two = pack[:part], pack[part + chans :]
        mains.append((jnp.where(upper, two, one), jnp.where(upper, one, two)))
        spreads.append(pack[part : part + chans])

    tokens = [
        ref[at : at + chans] if ref.shape[1] == lanes else ref[:, 2 * at : 2 * at + lanes]
        for ref in token_refs
        for at in (0, chans)
    ]
    tokens = jnp.concatenate(tokens + [own_ref[...]], 1)
    wide = tokens.astype(f32)
    spread = dot(jnp.concatenate(spreads, 0), jnp.concatenate([tokens, tokens], 0))
    row = lax.broadcasted_iota(jnp.int32, (part - chans, size + rows), 0)
    one = jnp.where(row == 0, 1.0, 0.0).astype(bf16)
    logits = []
    for slot, heads in enumerate(mains):
        product = spread[slot * chans : (slot + 1) * chans] * wide
        variance = jnp.maximum(jnp.sum(product, 0, keepdims=True), 0.0)
        normed = wide * lax.rsqrt(variance + norm_eps)
        high = normed.astype(bf16)
        low = (normed - high.astype(f32)).astype(bf16)
        features = jnp.concatenate([high, one, low, jnp.zeros_like(one)], 0)
        keys_ref[slot] = features[:, :size]
        own = features[:, size:]
        own_high = jnp.concatenate([own[:part], jnp.zeros((lanes - part, rows), bf16)], 0)
        for main in heads:
            ask = dot(jnp.concatenate([main, main], 0), own, (0, 0))[:chans].astype(bf16)
            shared = jnp.broadcast_to(dot(main[chans:], own_high)[1:2], (part - chans, rows))
            shared = jnp.where(row[:, :rows] == 0, shared, 0.0).astype(bf16)
            queries = jnp.concatenate([ask, shared, ask, jnp.zeros_like(shared)], 0)
            logits.append(dot(queries, keys_ref[slot], (0, 0)))

    total = None
    for place, scores in enumerate(logits):
        slot, head = divmod(place, 2)
        peak = jnp.broadcast_to(jnp.max(scores, 1, keepdims=True), (rows, lanes))
        if before:
            old_peak = refs[6 + count][place]
            peak = jnp.maximum(peak, old_peak)
        expo = jnp.exp2(scores - jnp.concatenate([peak] * (size // lanes), 1)).astype(bf16)
        mixed = dot(expo, keys_ref[slot], (1, 1))
        if before:
            factor = jnp.exp2(old_peak - peak)
            factor = jnp.concatenate([factor, factor[:, : 2 * part - lanes]], 1)
            mixed += refs[5 + count][place] * factor
        if last:
            mixed = (mixed / mixed[:, chans : chans + 1]).astype(bf16)
            main = jnp.concatenate([mains[slot][head]] * 2, 0)
            term = terms[slot][1] * dot(main, mixed, (0, 1))[chans:]
            total = term if total is None else total + term
        else:
            refs[-3][place] = mixed
            refs[-2][place] = peak
    if last:
        refs[-2][...] = total.astype(bf16)


def attend(terms, packs, own, tokens, state=(), last=True):
    rows = own.shape[1]
    count = len(tokens)
    pairs = 2 * count * rows * rows * len(terms)
    shape = [
        jax.ShapeDtypeStruct((2 * len(terms), rows, 2 * part), f32),
        jax.ShapeDtypeStruct((2 * len(terms), rows, lanes), f32),
    ]
    if last:
        shape = jax.ShapeDtypeStruct(own.shape, bf16)
    return pl.pallas_call(
        functools.partial(attend_kernel, terms, count, bool(state), last),
        out_shape=shape,
        scratch_shapes=[pltpu.VMEM((len(terms), 2 * part, count * rows), bf16)],
        compiler_params=pltpu.CompilerParams(vmem_limit_bytes=48 * 1024 * 1024),
        cost_estimate=pl.CostEstimate(
            flops=16 * pairs * lanes, bytes_accessed=1_000_000, transcendentals=pairs
        ),
        name="attend",
    )(*packs, own, *tokens, *state)


def swap(value, axis, flip, cross=0):
    axes = (axis, "tp")
    flip = 2 * flip + cross
    return lax.ppermute(value, axes, [(i, i ^ flip) for i in range(lax.axis_size(axes))])


def swap_all(value, axis, cross):
    one, three, two = (
        swap(value, axis, flip, crossed)
        for flip, crossed in ((1, cross[0]), (3, cross[2]), (2, cross[1]))
    )
    return [value, one, two, three]


def halve(tokens):
    return jnp.concatenate([tokens[:, :lanes], tokens[:, lanes:]], 0)


def other_core(value):
    return lax.ppermute(value, "tp", [(0, 1), (1, 0)])


def add_over(value, axis):
    sent = lax.optimization_barrier(value.astype(bf16))
    parts = [part.astype(f32) for part in swap_all(sent, axis, (1, 0, 1))]
    return (parts[0] + parts[1]) + (parts[2] + parts[3])


def add_heads(value):
    return add_over(add_over(value, "y"), "x")


def shards(
    latent_noise, score_noise, gen_step, score_step, embed_weight, qkv_weight, mod_weight, head_out
):
    chans = latent_noise.shape[1]
    gen_sigma = gen_step[0].astype(f32) / step_scale
    score_sigma = score_step[0].astype(f32) / step_scale
    latents, noise = latent_noise.T, score_noise.T
    odd = (lax.axis_index("x") + lax.axis_index("y")) % 2 == 1

    one = swap(latents, "mp", 1, 1)
    noise = jnp.where(odd, other_core(noise), noise)
    pack = fold_maps(
        gen_step, score_step, head_out[0, 0].T, embed_weight[0], mod_weight[0], qkv_weight[0, 0]
    )
    pack, latents, one, noise = lax.optimization_barrier((pack, latents, one, noise))
    pack = jnp.concatenate([pack, swap(pack[:part], "zh", 1, 1)], 0)
    two = halve(swap(latents, "mp", 2, 1))
    second = lax.axis_index("tp") == 1
    rows = pack.shape[0] // 2
    half = jnp.where(second, pack[rows:], pack[:rows])
    others = [
        swap(jnp.concatenate([half, two], 0), "mp", 1, 1),
        swap(half, "mp", 2, 1),
        swap(half, "mp", 3, 1),
    ]
    others = lax.optimization_barrier(others)
    near = [halve(latents), halve(one), two, others[0][rows:]]
    mine = jnp.concatenate(near + [other[:rows] for other in others], 0)
    theirs = other_core(mine)
    far = [theirs[at : at + lanes] for at in range(0, 4 * lanes, lanes)]
    packs = [pack]
    for at in range(4 * lanes, mine.shape[0], rows):
        here, there = mine[at : at + rows], theirs[at : at + rows]
        packs.append(
            jnp.concatenate([jnp.where(second, here, there), jnp.where(second, there, here)], 0)
        )

    latents = jnp.where(odd, jnp.concatenate([far[0][:chans], far[0][chans:]], 1), latents)
    speed = add_heads(attend(((0, 1.0),), packs, latents, near + far))
    clean = latents.astype(f32) - gen_sigma * speed
    noisy = (1.0 - score_sigma) * clean + score_sigma * noise.astype(f32)
    near = swap_all(noisy.astype(bf16), "mp", (1, 1, 1))
    far = other_core(jnp.stack(near))
    terms = ((1, 1.0), (2, -2.0), (3, 1.0))
    state = attend(terms, packs, near[0], near, last=False)
    grad = attend(terms, packs, near[0], list(far), state)
    grad = add_heads(grad) * -score_sigma
    grad = jnp.where(odd, other_core(grad), grad)
    clean = clean.astype(bf16)
    clean = jnp.where(odd, other_core(clean), clean)
    return (clean.T, grad.T)


def solution(mesh):
    models, heads, cores = mesh.devices.shape
    fine = Mesh(mesh.devices.reshape(models, 4, heads // 16, 4, cores), ("mp", "x", "zh", "y", "tp"))
    placed = (
        P(("mp", "tp"), None),
        P(("mp", "tp"), None),
        P(),
        P(),
        P("mp", None, None),
        P("mp", ("x", "zh", "y"), None, None),
        P("mp", None, None),
        P("mp", ("x", "zh", "y"), None, None),
    )
    return jax.shard_map(
        shards,
        mesh=fine,
        in_specs=placed,
        out_specs=(P(("mp", "tp"), None), P(("mp", "tp"), None)),
        check_vma=False,
    )
```

```python
import functools
import math

import jax
import jax.numpy as jnp
from jax import lax
from jax.experimental import pallas as pl
from jax.experimental.pallas import tpu as pltpu
from jax.sharding import Mesh
from jax.sharding import PartitionSpec as P

norm_eps = 1e-06
step_scale = 1000.0
f32 = jnp.float32
bf16 = jnp.bfloat16
chunk = 1024
lanes = 128
part = 80


def frequencies(freq_count):
    half_freq = freq_count // 2
    index = lax.broadcasted_iota(jnp.int32, (1, half_freq), 1)
    total = jnp.ones((1, half_freq), f32)
    for bit in range(half_freq.bit_length() - 1):
        factor = 10000.0 ** (-2.0 * (1 << bit) / freq_count)
        total = total * jnp.where((index >> bit) & 1 == 1, factor, 1.0)
    return total


def cos_sin(angle):
    turn = jnp.floor(angle * (2.0 / math.pi) + 0.5)
    left = angle - turn * 1.5703125
    left = left - turn * 4.837512969970703125e-4
    left = left - turn * 7.54978995489188216e-8
    square = left * left
    sine = left + left * square * (
        -1.6666654611e-1 + square * (8.3321608736e-3 - square * 1.9515295891e-4)
    )
    cosine = (
        1.0
        - 0.5 * square
        + square
        * square
        * (4.166664568298827e-2 + square * (-1.388731625493765e-3 + square * 2.443315711809948e-5))
    )
    quarter = turn.astype(jnp.int32) & 3
    odd = (quarter & 1) == 1
    cos_out = jnp.where(odd, sine, cosine)
    sin_out = jnp.where(odd, cosine, sine)
    cos_out = jnp.where((quarter == 1) | (quarter == 2), -cos_out, cos_out)
    sin_out = jnp.where(quarter >= 2, -sin_out, sin_out)
    return cos_out, sin_out


def dot(a, b, dims=(1, 0), precision=None):
    return lax.dot_general(
        a, b, (((dims[0],), (dims[1],)), ((), ())), precision=precision, preferred_element_type=f32
    )


def halves(value):
    high = value.astype(bf16)
    return high, (value - high.astype(f32)).astype(bf16)


def dot_halves(a, b):
    a_high, a_low = halves(a)
    b_high, b_low = halves(b)
    return dot(
        jnp.concatenate([a_high, a_high, a_low], 0),
        jnp.concatenate([b_high, b_low, b_high], 0),
        (0, 0),
    )


def maps_kernel(
    gen_ref, score_ref, embed_hbm, head_hbm, mod_hbm, weight_hbm, out_ref,
    embed_ref, head_ref, mod_ref, weight_ref, sems,
):
    chans, head_size = head_ref.shape
    width = embed_ref.shape[1]
    steps = width // chunk
    small = [
        pltpu.make_async_copy(source, target, sems.at[at])
        for at, (source, target) in enumerate(
            ((embed_hbm, embed_ref), (head_hbm, head_ref))
        )
    ]
    for copy in small:
        copy.start()
    copies = []
    for step in range(steps):
        mine = []
        for kind, (source, target, offset) in enumerate(
            ((mod_hbm, mod_ref, 0), (mod_hbm, mod_ref, width), (weight_hbm, weight_ref, 0))
        ):
            at = pl.ds(offset + step * chunk, chunk)
            copy = pltpu.make_async_copy(
                source.at[:, at], target.at[:, at], sems.at[2 + 3 * step + kind]
            )
            copy.start()
            mine.append(copy)
        copies.append(mine)

    small[0].wait()
    mean = jnp.sum(embed_ref[...].astype(f32), 1, keepdims=True) * (1.0 / width)
    ones = jnp.ones((part - chans, chunk), bf16)
    row_at = lax.broadcasted_iota(jnp.int32, (lanes - chans, chunk), 0)
    own_step = jnp.where(lax.axis_index("mp") == 0, gen_ref[0], score_ref[0]).astype(f32)
    waves = cos_sin(frequencies(2 * lanes) * own_step)
    freq = jnp.concatenate([jnp.broadcast_to(wave, (lanes, lanes)).T for wave in waves], 0)
    maps = gram = None
    for step in range(steps):
        own = embed_ref[:, pl.ds(step * chunk, chunk)]
        gram_term = dot(jnp.concatenate([own, ones], 0), own, (1, 1))
        rows = []
        copies[step][0].wait()
        copies[step][1].wait()
        for kind in range(2):
            total = None
            for at in range(0, freq.shape[0], 16):
                here = mod_ref[at : at + 16, pl.ds(kind * width + step * chunk, chunk)]
                scale = jnp.concatenate([freq[at : at + 16]] * (chunk // lanes), 1)
                term = here.astype(f32) * scale
                total = term if total is None else total + term
            rows.append(jnp.sum(total, 0, keepdims=True))
        centred = (own.astype(f32) - mean) * (1.0 + rows[1])
        tail = jnp.where(row_at == 0, jnp.broadcast_to(rows[0], row_at.shape), 0.0)
        lifted = jnp.concatenate([centred.astype(bf16), tail.astype(bf16)], 0)
        copies[step][2].wait()
        maps_term = dot(weight_ref[:, pl.ds(step * chunk, chunk)], lifted, (1, 1))
        maps = maps_term if maps is None else maps + maps_term
        gram = gram_term if gram is None else gram + gram_term

    map_q = maps[:head_size] * (head_size ** (-0.5) * math.log2(math.e))
    map_k = maps[head_size : 2 * head_size]
    map_v = maps[2 * head_size :]
    lane = lax.broadcasted_iota(jnp.int32, (head_size, lanes), 1)
    small[1].wait()
    wide_head = jnp.concatenate([jnp.zeros_like(head_ref), head_ref[...]], 0)
    main = dot_halves(map_q, jnp.where(lane < chans, map_k, 0.0))
    high, low = halves(map_v)
    main += dot(high, wide_head, (0, 1)) + dot(low, wide_head, (0, 1))
    last = dot_halves(map_k, map_q)[chans : chans + 1]
    main = main[:part]
    row = lax.broadcasted_iota(jnp.int32, main.shape, 0)
    main = jnp.where(row == chans + 1, jnp.broadcast_to(last, main.shape), main)
    out_ref[:part] = main.astype(bf16)
    gram = gram * (1.0 / width)
    high, low = halves(gram[:chans] - mean * gram[chans : chans + 1])
    out_ref[part:] = jnp.concatenate([high.astype(f32), low.astype(f32)], 1).astype(bf16)


def fold_maps(gen_step, score_step, head, embed, mod_weight, weight):
    chans, width = embed.shape
    return pl.pallas_call(
        maps_kernel,
        in_specs=[pl.BlockSpec(memory_space=pltpu.SMEM)] * 2
        + [pl.BlockSpec(memory_space=pl.ANY)] * 4,
        out_specs=pl.BlockSpec(memory_space=pltpu.VMEM),
        out_shape=jax.ShapeDtypeStruct((part + chans, lanes), bf16),
        scratch_shapes=[
            pltpu.VMEM(embed.shape, bf16),
            pltpu.VMEM(head.shape, bf16),
            pltpu.VMEM(mod_weight.shape, bf16),
            pltpu.VMEM(weight.shape, bf16),
            pltpu.SemaphoreType.DMA((2 + 3 * (width // chunk),)),
        ],
        compiler_params=pltpu.CompilerParams(vmem_limit_bytes=56_000_000),
        cost_estimate=pl.CostEstimate(
            flops=6_000_000_000, bytes_accessed=10_000_000, transcendentals=0
        ),
        name="fold_maps",
    )(gen_step, score_step, embed, head, mod_weight, weight)


def attend_kernel(terms, count, before, last, *refs):
    refs = list(refs)
    pack_refs, own_ref, token_refs = refs[:4], refs[4], refs[5 : 5 + count]
    keys_ref = refs[-1]
    chans, rows = own_ref.shape
    size = count * rows
    here, upper = lax.axis_index("mp"), lax.axis_index("zh") == 1

    mains, spreads = [], []
    for model, _ in terms:
        at = here ^ model
        pack = pack_refs[0][...]
        for other in range(1, 4):
            pack = jnp.where(at == other, pack_refs[other][...], pack)
        one, two = pack[:part], pack[part + chans :]
        mains.append((jnp.where(upper, two, one), jnp.where(upper, one, two)))
        spreads.append(pack[part : part + chans])

    tokens = jnp.concatenate([ref[...] for ref in token_refs] + [own_ref[...]], 1)
    wide = tokens.astype(f32)
    spread = dot(jnp.concatenate(spreads, 0), jnp.concatenate([tokens, tokens], 0))
    row = lax.broadcasted_iota(jnp.int32, (part - chans, size + rows), 0)
    one = jnp.where(row == 0, 1.0, 0.0).astype(bf16)
    logits = []
    for slot, heads in enumerate(mains):
        product = spread[slot * chans : (slot + 1) * chans] * wide
        variance = jnp.maximum(jnp.sum(product, 0, keepdims=True), 0.0)
        normed = wide * lax.rsqrt(variance + norm_eps)
        high = normed.astype(bf16)
        low = (normed - high.astype(f32)).astype(bf16)
        features = jnp.concatenate([high, one, low, jnp.zeros_like(one)], 0)
        keys_ref[slot] = features[:, :size]
        own = features[:, size:]
        own_high = jnp.concatenate([own[:part], jnp.zeros((lanes - part, rows), bf16)], 0)
        for main in heads:
            ask = dot(jnp.concatenate([main, main], 0), own, (0, 0))[:chans].astype(bf16)
            shared = jnp.broadcast_to(dot(main[chans:], own_high)[1:2], (part - chans, rows))
            shared = jnp.where(row[:, :rows] == 0, shared, 0.0).astype(bf16)
            queries = jnp.concatenate([ask, shared, ask, jnp.zeros_like(shared)], 0)
            logits.append(dot(queries, keys_ref[slot], (0, 0)))

    total = None
    unit = lax.broadcasted_iota(jnp.int32, (part, lanes), 1) == 0
    pick = lax.broadcasted_iota(jnp.int32, (part, lanes), 0) == chans
    pick = jnp.where(pick, 1.0, 0.0).astype(bf16)
    for place, scores in enumerate(logits):
        slot, head = divmod(place, 2)
        peak = jnp.broadcast_to(jnp.max(scores, 1, keepdims=True), (rows, lanes))
        if before:
            old_peak = refs[6 + count][place]
            peak = jnp.maximum(peak, old_peak)
        expo = jnp.exp2(scores - jnp.concatenate([peak] * (size // lanes), 1)).astype(bf16)
        mixed = dot(expo, keys_ref[slot], (1, 1))
        if before:
            factor = jnp.exp2(old_peak - peak)
            factor = jnp.concatenate([factor, factor[:, : 2 * part - lanes]], 1)
            mixed += refs[5 + count][place] * factor
        if last:
            main = jnp.concatenate([jnp.where(unit, pick, mains[slot][head])] * 2, 0)
            term = dot(main, mixed.astype(bf16), (0, 1))
            term = term[chans:] * (terms[slot][1] / term[:1])
            total = term if total is None else total + term
        else:
            refs[-3][place] = mixed
            refs[-2][place] = peak
    if last:
        refs[-2][...] = total.astype(bf16)


def attend(terms, packs, own, tokens, state=(), last=True):
    rows = own.shape[1]
    count = len(tokens)
    pairs = 2 * count * rows * rows * len(terms)
    shape = [
        jax.ShapeDtypeStruct((2 * len(terms), rows, 2 * part), f32),
        jax.ShapeDtypeStruct((2 * len(terms), rows, lanes), f32),
    ]
    if last:
        shape = jax.ShapeDtypeStruct(own.shape, bf16)
    return pl.pallas_call(
        functools.partial(attend_kernel, terms, count, bool(state), last),
        out_shape=shape,
        scratch_shapes=[pltpu.VMEM((len(terms), 2 * part, count * rows), bf16)],
        compiler_params=pltpu.CompilerParams(vmem_limit_bytes=48 * 1024 * 1024),
        cost_estimate=pl.CostEstimate(
            flops=16 * pairs * lanes, bytes_accessed=1_000_000, transcendentals=pairs
        ),
        name="attend",
    )(*packs, own, *tokens, *state)


def swap(value, axis, flip, cross=0):
    axes = (axis, "tp")
    flip = 2 * flip + cross
    return lax.ppermute(value, axes, [(i, i ^ flip) for i in range(lax.axis_size(axes))])


def swap_all(value, axis, cross):
    one, three, two = (
        swap(value, axis, flip, crossed)
        for flip, crossed in ((1, cross[0]), (3, cross[2]), (2, cross[1]))
    )
    return [value, one, two, three]


def other_core(value):
    return lax.ppermute(value, "tp", [(0, 1), (1, 0)])


def add_over(value, axis):
    sent = lax.optimization_barrier(value.astype(bf16))
    parts = [part.astype(f32) for part in swap_all(sent, axis, (1, 0, 1))]
    return (parts[0] + parts[1]) + (parts[2] + parts[3])


def add_heads(value):
    return add_over(add_over(value, "y"), "x")


def shards(
    latent_noise, score_noise, gen_step, score_step, embed_weight, qkv_weight, mod_weight, head_out
):
    model = lax.axis_index("mp")
    gen_sigma = gen_step[0].astype(f32) / step_scale
    score_sigma = score_step[0].astype(f32) / step_scale
    latents, noise = latent_noise.T, score_noise.T
    odd = (lax.axis_index("x") + lax.axis_index("y")) % 2 == 1

    first = swap(latents, "mp", 1, 1)
    noise = jnp.where(odd, other_core(noise), noise)
    pack = fold_maps(
        gen_step, score_step, head_out[0, 0].T, embed_weight[0], mod_weight[0], qkv_weight[0, 0]
    )
    pack, first, noise = lax.optimization_barrier((pack, first, noise))
    other = swap(pack[:part], "zh", 1, 1)
    pair = swap(jnp.stack([latents, first]), "mp", 2, 1)
    packs = swap_all(jnp.concatenate([pack, other], 0), "mp", (1, 1, 1))
    near = [latents, first, pair[0], pair[1]]
    far = other_core(jnp.stack(near))

    latents = jnp.where(odd, far[0], latents)
    speed = add_heads(attend(((0, 1.0),), packs, latents, near + list(far)))
    clean = latents.astype(f32) - gen_sigma * speed
    noisy = (1.0 - score_sigma) * clean + score_sigma * noise.astype(f32)
    near = swap_all(noisy.astype(bf16), "mp", (1, 1, 1))
    far = other_core(jnp.stack(near))
    terms = ((1, 1.0), (2, -2.0), (3, 1.0))
    state = attend(terms, packs, near[0], near, last=False)
    grad = attend(terms, packs, near[0], list(far), state)
    grad = add_heads(grad) * -score_sigma
    grad = jnp.where(odd, other_core(grad), grad)
    clean = clean.astype(bf16)
    clean = jnp.where(odd, other_core(clean), clean)
    return (clean.T, grad.T)


def solution(mesh):
    models, heads, cores = mesh.devices.shape
    fine = Mesh(mesh.devices.reshape(models, 4, heads // 16, 4, cores), ("mp", "x", "zh", "y", "tp"))
    placed = (
        P(("mp", "tp"), None),
        P(("mp", "tp"), None),
        P(),
        P(),
        P("mp", None, None),
        P("mp", ("x", "zh", "y"), None, None),
        P("mp", None, None),
        P("mp", ("x", "zh", "y"), None, None),
    )
    return jax.shard_map(
        shards,
        mesh=fine,
        in_specs=placed,
        out_specs=(P(("mp", "tp"), None), P(("mp", "tp"), None)),
        check_vma=False,
    )
```

```python
import functools
import math

import jax
import jax.numpy as jnp
from jax import lax
from jax.experimental import pallas as pl
from jax.experimental.pallas import tpu as pltpu
from jax.sharding import Mesh
from jax.sharding import PartitionSpec as P

norm_eps = 1e-06
step_scale = 1000.0
f32 = jnp.float32
bf16 = jnp.bfloat16
chunk = 1024
lanes = 128
part = 80


def frequencies(freq_count):
    half_freq = freq_count // 2
    index = lax.broadcasted_iota(jnp.int32, (1, half_freq), 1)
    total = jnp.ones((1, half_freq), f32)
    for bit in range(half_freq.bit_length() - 1):
        factor = 10000.0 ** (-2.0 * (1 << bit) / freq_count)
        total = total * jnp.where((index >> bit) & 1 == 1, factor, 1.0)
    return total


def cos_sin(angle):
    turn = jnp.floor(angle * (2.0 / math.pi) + 0.5)
    left = angle - turn * 1.5703125
    left = left - turn * 4.837512969970703125e-4
    left = left - turn * 7.54978995489188216e-8
    square = left * left
    sine = left + left * square * (
        -1.6666654611e-1 + square * (8.3321608736e-3 - square * 1.9515295891e-4)
    )
    cosine = (
        1.0
        - 0.5 * square
        + square
        * square
        * (4.166664568298827e-2 + square * (-1.388731625493765e-3 + square * 2.443315711809948e-5))
    )
    quarter = turn.astype(jnp.int32) & 3
    odd = (quarter & 1) == 1
    cos_out = jnp.where(odd, sine, cosine)
    sin_out = jnp.where(odd, cosine, sine)
    cos_out = jnp.where((quarter == 1) | (quarter == 2), -cos_out, cos_out)
    sin_out = jnp.where(quarter >= 2, -sin_out, sin_out)
    return cos_out, sin_out


def dot(a, b, dims=(1, 0), precision=None):
    return lax.dot_general(
        a, b, (((dims[0],), (dims[1],)), ((), ())), precision=precision, preferred_element_type=f32
    )


def halves(value):
    high = value.astype(bf16)
    return high, (value - high.astype(f32)).astype(bf16)


def dot_halves(a, b):
    a_high, a_low = halves(a)
    b_high, b_low = halves(b)
    return dot(
        jnp.concatenate([a_high, a_high, a_low], 0),
        jnp.concatenate([b_high, b_low, b_high], 0),
        (0, 0),
    )


def maps_kernel(
    gen_ref, score_ref, embed_hbm, head_hbm, mod_hbm, weight_hbm, out_ref,
    embed_ref, head_ref, mod_ref, weight_ref, sems,
):
    chans, head_size = head_ref.shape
    width = embed_ref.shape[1]
    steps = width // chunk
    small = [
        pltpu.make_async_copy(source, target, sems.at[at])
        for at, (source, target) in enumerate(
            ((embed_hbm, embed_ref), (head_hbm, head_ref))
        )
    ]
    for copy in small:
        copy.start()
    copies = []
    for step in range(steps):
        mine = []
        for kind, (source, target, offset) in enumerate(
            ((mod_hbm, mod_ref, 0), (mod_hbm, mod_ref, width), (weight_hbm, weight_ref, 0))
        ):
            at = pl.ds(offset + step * chunk, chunk)
            copy = pltpu.make_async_copy(
                source.at[:, at], target.at[:, at], sems.at[2 + 3 * step + kind]
            )
            copy.start()
            mine.append(copy)
        copies.append(mine)

    small[0].wait()
    mean = jnp.sum(embed_ref[...].astype(f32), 1, keepdims=True) * (1.0 / width)
    ones = jnp.ones((part - chans, chunk), bf16)
    row_at = lax.broadcasted_iota(jnp.int32, (lanes - chans, chunk), 0)
    own_step = jnp.where(lax.axis_index("mp") == 0, gen_ref[0], score_ref[0]).astype(f32)
    waves = cos_sin(frequencies(2 * lanes) * own_step)
    freq = jnp.concatenate([jnp.broadcast_to(wave, (lanes, lanes)).T for wave in waves], 0)
    maps = gram = None
    for step in range(steps):
        own = embed_ref[:, pl.ds(step * chunk, chunk)]
        gram_term = dot(jnp.concatenate([own, ones], 0), own, (1, 1))
        rows = []
        copies[step][0].wait()
        copies[step][1].wait()
        for kind in range(2):
            total = None
            for at in range(0, freq.shape[0], 16):
                here = mod_ref[at : at + 16, pl.ds(kind * width + step * chunk, chunk)]
                scale = jnp.concatenate([freq[at : at + 16]] * (chunk // lanes), 1)
                term = here.astype(f32) * scale
                total = term if total is None else total + term
            rows.append(jnp.sum(total, 0, keepdims=True))
        centred = (own.astype(f32) - mean) * (1.0 + rows[1])
        tail = jnp.where(row_at == 0, jnp.broadcast_to(rows[0], row_at.shape), 0.0)
        lifted = jnp.concatenate([centred.astype(bf16), tail.astype(bf16)], 0)
        copies[step][2].wait()
        maps_term = dot(weight_ref[:, pl.ds(step * chunk, chunk)], lifted, (1, 1))
        maps = maps_term if maps is None else maps + maps_term
        gram = gram_term if gram is None else gram + gram_term

    map_q = maps[:head_size] * (head_size ** (-0.5) * math.log2(math.e))
    map_k = maps[head_size : 2 * head_size]
    map_v = maps[2 * head_size :]
    lane = lax.broadcasted_iota(jnp.int32, (head_size, lanes), 1)
    small[1].wait()
    wide_head = jnp.concatenate([jnp.zeros_like(head_ref), head_ref[...]], 0)
    main = dot_halves(map_q, jnp.where(lane < chans, map_k, 0.0))
    high, low = halves(map_v)
    main += dot(high, wide_head, (0, 1)) + dot(low, wide_head, (0, 1))
    last = dot_halves(map_k, map_q)[chans : chans + 1]
    main = main[:part]
    row = lax.broadcasted_iota(jnp.int32, main.shape, 0)
    main = jnp.where(row == chans + 1, jnp.broadcast_to(last, main.shape), main)
    out_ref[:part] = main.astype(bf16)
    gram = gram * (1.0 / width)
    high, low = halves(gram[:chans] - mean * gram[chans : chans + 1])
    out_ref[part:] = jnp.concatenate([high.astype(f32), low.astype(f32)], 1).astype(bf16)


def fold_maps(gen_step, score_step, head, embed, mod_weight, weight):
    chans, width = embed.shape
    return pl.pallas_call(
        maps_kernel,
        in_specs=[pl.BlockSpec(memory_space=pltpu.SMEM)] * 2
        + [pl.BlockSpec(memory_space=pl.ANY)] * 4,
        out_specs=pl.BlockSpec(memory_space=pltpu.VMEM),
        out_shape=jax.ShapeDtypeStruct((part + chans, lanes), bf16),
        scratch_shapes=[
            pltpu.VMEM(embed.shape, bf16),
            pltpu.VMEM(head.shape, bf16),
            pltpu.VMEM(mod_weight.shape, bf16),
            pltpu.VMEM(weight.shape, bf16),
            pltpu.SemaphoreType.DMA((2 + 3 * (width // chunk),)),
        ],
        compiler_params=pltpu.CompilerParams(vmem_limit_bytes=56_000_000),
        cost_estimate=pl.CostEstimate(
            flops=6_000_000_000, bytes_accessed=10_000_000, transcendentals=0
        ),
        name="fold_maps",
    )(gen_step, score_step, embed, head, mod_weight, weight)


def attend_kernel(terms, count, before, last, *refs):
    refs = list(refs)
    pack_refs, own_ref, token_refs = refs[:4], refs[4], refs[5 : 5 + count]
    keys_ref = refs[-1]
    chans, rows = own_ref.shape
    size = count * rows
    here, upper = lax.axis_index("mp"), lax.axis_index("zh") == 1

    mains, spreads = [], []
    for model, _ in terms:
        at = here ^ model
        pack = pack_refs[0][...]
        for other in range(1, 4):
            pack = jnp.where(at == other, pack_refs[other][...], pack)
        one, two = pack[:part], pack[part + chans :]
        mains.append((jnp.where(upper, two, one), jnp.where(upper, one, two)))
        spreads.append(pack[part : part + chans])

    tokens = jnp.concatenate([ref[...] for ref in token_refs] + [own_ref[...]], 1)
    wide = tokens.astype(f32)
    spread = dot(jnp.concatenate(spreads, 0), jnp.concatenate([tokens, tokens], 0))
    row = lax.broadcasted_iota(jnp.int32, (part - chans, size + rows), 0)
    one = jnp.where(row == 0, 1.0, 0.0).astype(bf16)
    logits = []
    for slot, heads in enumerate(mains):
        product = spread[slot * chans : (slot + 1) * chans] * wide
        variance = jnp.maximum(jnp.sum(product, 0, keepdims=True), 0.0)
        normed = wide * lax.rsqrt(variance + norm_eps)
        high = normed.astype(bf16)
        low = (normed - high.astype(f32)).astype(bf16)
        features = jnp.concatenate([high, one, low, jnp.zeros_like(one)], 0)
        keys_ref[slot] = features[:, :size]
        own = features[:, size:]
        own_high = jnp.concatenate([own[:part], jnp.zeros((lanes - part, rows), bf16)], 0)
        for main in heads:
            ask = dot(jnp.concatenate([main, main], 0), own, (0, 0))[:chans].astype(bf16)
            shared = jnp.broadcast_to(dot(main[chans:], own_high)[1:2], (part - chans, rows))
            shared = jnp.where(row[:, :rows] == 0, shared, 0.0).astype(bf16)
            queries = jnp.concatenate([ask, shared, ask, jnp.zeros_like(shared)], 0)
            logits.append(dot(queries, keys_ref[slot], (0, 0)))

    total = None
    pick = lax.broadcasted_iota(jnp.int32, (part, lanes), 0) == chans
    pick = jnp.where(pick, 1.0, 0.0).astype(bf16)
    for place, scores in enumerate(logits):
        slot, head = divmod(place, 2)
        peak = jnp.broadcast_to(jnp.max(scores, 1, keepdims=True), (rows, lanes))
        if before:
            old_peak = refs[6 + count][place]
            peak = jnp.maximum(peak, old_peak)
        expo = jnp.exp2(scores - jnp.concatenate([peak] * (size // lanes), 1)).astype(bf16)
        mixed = dot(expo, keys_ref[slot], (1, 1))
        if before:
            factor = jnp.exp2(old_peak - peak)
            factor = jnp.concatenate([factor, factor[:, : 2 * part - lanes]], 1)
            mixed += refs[5 + count][place] * factor
        if last:
            main = jnp.concatenate([jnp.concatenate([mains[slot][head], pick], 1)] * 2, 0)
            term = dot(mixed.astype(bf16), main)
            term = term[:, :lanes] * (terms[slot][1] / term[:, lanes:])
            total = term if total is None else total + term
        else:
            refs[-3][place] = mixed
            refs[-2][place] = peak
    if last:
        refs[-2][...] = total.T[chans:].astype(bf16)


def attend(terms, packs, own, tokens, state=(), last=True):
    rows = own.shape[1]
    count = len(tokens)
    pairs = 2 * count * rows * rows * len(terms)
    shape = [
        jax.ShapeDtypeStruct((2 * len(terms), rows, 2 * part), f32),
        jax.ShapeDtypeStruct((2 * len(terms), rows, lanes), f32),
    ]
    if last:
        shape = jax.ShapeDtypeStruct(own.shape, bf16)
    return pl.pallas_call(
        functools.partial(attend_kernel, terms, count, bool(state), last),
        out_shape=shape,
        scratch_shapes=[pltpu.VMEM((len(terms), 2 * part, count * rows), bf16)],
        compiler_params=pltpu.CompilerParams(vmem_limit_bytes=48 * 1024 * 1024),
        cost_estimate=pl.CostEstimate(
            flops=16 * pairs * lanes, bytes_accessed=1_000_000, transcendentals=pairs
        ),
        name="attend",
    )(*packs, own, *tokens, *state)


def swap(value, axis, flip, cross=0):
    axes = (axis, "tp")
    flip = 2 * flip + cross
    return lax.ppermute(value, axes, [(i, i ^ flip) for i in range(lax.axis_size(axes))])


def swap_all(value, axis, cross):
    one, three, two = (
        swap(value, axis, flip, crossed)
        for flip, crossed in ((1, cross[0]), (3, cross[2]), (2, cross[1]))
    )
    return [value, one, two, three]


def other_core(value):
    return lax.ppermute(value, "tp", [(0, 1), (1, 0)])


def add_over(value, axis):
    sent = lax.optimization_barrier(value.astype(bf16))
    parts = [part.astype(f32) for part in swap_all(sent, axis, (1, 0, 1))]
    return (parts[0] + parts[1]) + (parts[2] + parts[3])


def add_heads(value):
    return add_over(add_over(value, "y"), "x")


def shards(
    latent_noise, score_noise, gen_step, score_step, embed_weight, qkv_weight, mod_weight, head_out
):
    model = lax.axis_index("mp")
    gen_sigma = gen_step[0].astype(f32) / step_scale
    score_sigma = score_step[0].astype(f32) / step_scale
    latents, noise = latent_noise.T, score_noise.T
    odd = (lax.axis_index("x") + lax.axis_index("y")) % 2 == 1

    first = swap(latents, "mp", 1, 1)
    noise = jnp.where(odd, other_core(noise), noise)
    pack = fold_maps(
        gen_step, score_step, head_out[0, 0].T, embed_weight[0], mod_weight[0], qkv_weight[0, 0]
    )
    pack, first, noise = lax.optimization_barrier((pack, first, noise))
    other = swap(pack[:part], "zh", 1, 1)
    pair = swap(jnp.stack([latents, first]), "mp", 2, 1)
    packs = swap_all(jnp.concatenate([pack, other], 0), "mp", (1, 1, 1))
    near = [latents, first, pair[0], pair[1]]
    far = other_core(jnp.stack(near))

    latents = jnp.where(odd, far[0], latents)
    speed = add_heads(attend(((0, 1.0),), packs, latents, near + list(far)))
    clean = latents.astype(f32) - gen_sigma * speed
    noisy = (1.0 - score_sigma) * clean + score_sigma * noise.astype(f32)
    near = swap_all(noisy.astype(bf16), "mp", (1, 1, 1))
    far = other_core(jnp.stack(near))
    terms = ((1, 1.0), (2, -2.0), (3, 1.0))
    state = attend(terms, packs, near[0], near, last=False)
    grad = attend(terms, packs, near[0], list(far), state)
    grad = add_heads(grad) * -score_sigma
    grad = jnp.where(odd, other_core(grad), grad)
    clean = clean.astype(bf16)
    clean = jnp.where(odd, other_core(clean), clean)
    return (clean.T, grad.T)


def solution(mesh):
    models, heads, cores = mesh.devices.shape
    fine = Mesh(mesh.devices.reshape(models, 4, heads // 16, 4, cores), ("mp", "x", "zh", "y", "tp"))
    placed = (
        P(("mp", "tp"), None),
        P(("mp", "tp"), None),
        P(),
        P(),
        P("mp", None, None),
        P("mp", ("x", "zh", "y"), None, None),
        P("mp", None, None),
        P("mp", ("x", "zh", "y"), None, None),
    )
    return jax.shard_map(
        shards,
        mesh=fine,
        in_specs=placed,
        out_specs=(P(("mp", "tp"), None), P(("mp", "tp"), None)),
        check_vma=False,
    )
```

```python
import functools
import math

import jax
import jax.numpy as jnp
from jax import lax
from jax.experimental import pallas as pl
from jax.experimental.pallas import tpu as pltpu
from jax.sharding import Mesh
from jax.sharding import PartitionSpec as P

norm_eps = 1e-06
step_scale = 1000.0
f32 = jnp.float32
bf16 = jnp.bfloat16
chunk = 1024
lanes = 128
part = 80


def frequencies(freq_count):
    half_freq = freq_count // 2
    index = lax.broadcasted_iota(jnp.int32, (1, half_freq), 1)
    total = jnp.ones((1, half_freq), f32)
    for bit in range(half_freq.bit_length() - 1):
        factor = 10000.0 ** (-2.0 * (1 << bit) / freq_count)
        total = total * jnp.where((index >> bit) & 1 == 1, factor, 1.0)
    return total


def cos_sin(angle):
    turn = jnp.floor(angle * (2.0 / math.pi) + 0.5)
    left = angle - turn * 1.5703125
    left = left - turn * 4.837512969970703125e-4
    left = left - turn * 7.54978995489188216e-8
    square = left * left
    sine = left + left * square * (
        -1.6666654611e-1 + square * (8.3321608736e-3 - square * 1.9515295891e-4)
    )
    cosine = (
        1.0
        - 0.5 * square
        + square
        * square
        * (4.166664568298827e-2 + square * (-1.388731625493765e-3 + square * 2.443315711809948e-5))
    )
    quarter = turn.astype(jnp.int32) & 3
    odd = (quarter & 1) == 1
    cos_out = jnp.where(odd, sine, cosine)
    sin_out = jnp.where(odd, cosine, sine)
    cos_out = jnp.where((quarter == 1) | (quarter == 2), -cos_out, cos_out)
    sin_out = jnp.where(quarter >= 2, -sin_out, sin_out)
    return cos_out, sin_out


def dot(a, b, dims=(1, 0), precision=None):
    return lax.dot_general(
        a, b, (((dims[0],), (dims[1],)), ((), ())), precision=precision, preferred_element_type=f32
    )


def halves(value):
    high = value.astype(bf16)
    return high, (value - high.astype(f32)).astype(bf16)


def dot_halves(a, b):
    a_high, a_low = halves(a)
    b_high, b_low = halves(b)
    return dot(
        jnp.concatenate([a_high, a_high, a_low], 0),
        jnp.concatenate([b_high, b_low, b_high], 0),
        (0, 0),
    )


def maps_kernel(
    gen_ref, score_ref, embed_hbm, head_hbm, mod_hbm, weight_hbm, out_ref,
    embed_ref, head_ref, mod_ref, weight_ref, sems,
):
    chans, head_size = head_ref.shape
    width = embed_ref.shape[1]
    steps = width // chunk
    small = [
        pltpu.make_async_copy(source, target, sems.at[at])
        for at, (source, target) in enumerate(
            ((embed_hbm, embed_ref), (head_hbm, head_ref))
        )
    ]
    for copy in small:
        copy.start()
    copies = []
    for step in range(steps):
        mine = []
        for kind, (source, target, offset) in enumerate(
            ((mod_hbm, mod_ref, 0), (mod_hbm, mod_ref, width), (weight_hbm, weight_ref, 0))
        ):
            at = pl.ds(offset + step * chunk, chunk)
            copy = pltpu.make_async_copy(
                source.at[:, at], target.at[:, at], sems.at[2 + 3 * step + kind]
            )
            copy.start()
            mine.append(copy)
        copies.append(mine)

    small[0].wait()
    mean = jnp.sum(embed_ref[...].astype(f32), 1, keepdims=True) * (1.0 / width)
    ones = jnp.ones((part - chans, chunk), bf16)
    row_at = lax.broadcasted_iota(jnp.int32, (lanes - chans, chunk), 0)
    own_step = jnp.where(lax.axis_index("mp") == 0, gen_ref[0], score_ref[0]).astype(f32)
    waves = cos_sin(frequencies(2 * lanes) * own_step)
    freq = jnp.concatenate([jnp.broadcast_to(wave, (lanes, lanes)).T for wave in waves], 0)
    maps = gram = None
    for step in range(steps):
        own = embed_ref[:, pl.ds(step * chunk, chunk)]
        gram_term = dot(jnp.concatenate([own, ones], 0), own, (1, 1))
        rows = []
        copies[step][0].wait()
        copies[step][1].wait()
        for kind in range(2):
            total = None
            for at in range(0, freq.shape[0], 16):
                here = mod_ref[at : at + 16, pl.ds(kind * width + step * chunk, chunk)]
                scale = jnp.concatenate([freq[at : at + 16]] * (chunk // lanes), 1)
                term = here.astype(f32) * scale
                total = term if total is None else total + term
            rows.append(jnp.sum(total, 0, keepdims=True))
        centred = (own.astype(f32) - mean) * (1.0 + rows[1])
        tail = jnp.where(row_at == 0, jnp.broadcast_to(rows[0], row_at.shape), 0.0)
        lifted = jnp.concatenate([centred.astype(bf16), tail.astype(bf16)], 0)
        copies[step][2].wait()
        maps_term = dot(weight_ref[:, pl.ds(step * chunk, chunk)], lifted, (1, 1))
        maps = maps_term if maps is None else maps + maps_term
        gram = gram_term if gram is None else gram + gram_term

    map_q = maps[:head_size] * (head_size ** (-0.5) * math.log2(math.e))
    map_k = maps[head_size : 2 * head_size]
    map_v = maps[2 * head_size :]
    lane = lax.broadcasted_iota(jnp.int32, (head_size, lanes), 1)
    small[1].wait()
    wide_head = jnp.concatenate([jnp.zeros_like(head_ref), head_ref[...]], 0)
    main = dot_halves(map_q, jnp.where(lane < chans, map_k, 0.0))
    high, low = halves(map_v)
    main += dot(high, wide_head, (0, 1)) + dot(low, wide_head, (0, 1))
    last = dot_halves(map_k, map_q)[chans : chans + 1]
    main = main[:part]
    row = lax.broadcasted_iota(jnp.int32, main.shape, 0)
    main = jnp.where(row == chans + 1, jnp.broadcast_to(last, main.shape), main)
    out_ref[:part] = main.astype(bf16)
    gram = gram * (1.0 / width)
    high, low = halves(gram[:chans] - mean * gram[chans : chans + 1])
    out_ref[part:] = jnp.concatenate([high.astype(f32), low.astype(f32)], 1).astype(bf16)


def fold_maps(gen_step, score_step, head, embed, mod_weight, weight):
    chans, width = embed.shape
    return pl.pallas_call(
        maps_kernel,
        in_specs=[pl.BlockSpec(memory_space=pltpu.SMEM)] * 2
        + [pl.BlockSpec(memory_space=pl.ANY)] * 4,
        out_specs=pl.BlockSpec(memory_space=pltpu.VMEM),
        out_shape=jax.ShapeDtypeStruct((part + chans, lanes), bf16),
        scratch_shapes=[
            pltpu.VMEM(embed.shape, bf16),
            pltpu.VMEM(head.shape, bf16),
            pltpu.VMEM(mod_weight.shape, bf16),
            pltpu.VMEM(weight.shape, bf16),
            pltpu.SemaphoreType.DMA((2 + 3 * (width // chunk),)),
        ],
        compiler_params=pltpu.CompilerParams(vmem_limit_bytes=56_000_000),
        cost_estimate=pl.CostEstimate(
            flops=6_000_000_000, bytes_accessed=10_000_000, transcendentals=0
        ),
        name="fold_maps",
    )(gen_step, score_step, embed, head, mod_weight, weight)


def attend_kernel(terms, count, before, last, *refs):
    refs = list(refs)
    pack_refs, own_ref, token_refs = refs[:4], refs[4], refs[5 : 5 + count]
    keys_ref = refs[-1]
    chans, rows = own_ref.shape
    size = count * rows
    here, upper = lax.axis_index("mp"), lax.axis_index("zh") == 1

    mains, spreads = [], []
    for model, _ in terms:
        at = here ^ model
        pack = pack_refs[0][...]
        for other in range(1, 4):
            pack = jnp.where(at == other, pack_refs[other][...], pack)
        one, two = pack[:part], pack[part + chans :]
        mains.append((jnp.where(upper, two, one), jnp.where(upper, one, two)))
        spreads.append(pack[part : part + chans])

    tokens = jnp.concatenate([ref[...] for ref in token_refs] + [own_ref[...]], 1)
    wide = tokens.astype(f32)
    spread = dot(jnp.concatenate(spreads, 0), jnp.concatenate([tokens, tokens], 0))
    row = lax.broadcasted_iota(jnp.int32, (part - chans, size + rows), 0)
    one = jnp.where(row == 0, 1.0, 0.0).astype(bf16)
    logits = []
    for slot, heads in enumerate(mains):
        product = spread[slot * chans : (slot + 1) * chans] * wide
        variance = jnp.maximum(jnp.sum(product, 0, keepdims=True), 0.0)
        normed = wide * lax.rsqrt(variance + norm_eps)
        high = normed.astype(bf16)
        low = (normed - high.astype(f32)).astype(bf16)
        features = jnp.concatenate([high, one, low, jnp.zeros_like(one)], 0)
        keys_ref[slot] = features[:, :size]
        own = features[:, size:]
        own_high = jnp.concatenate([own[:part], jnp.zeros((lanes - part, rows), bf16)], 0)
        for main in heads:
            ask = dot(jnp.concatenate([main, main], 0), own, (0, 0))[:chans].astype(bf16)
            shared = jnp.broadcast_to(dot(main[chans:], own_high)[1:2], (part - chans, rows))
            shared = jnp.where(row[:, :rows] == 0, shared, 0.0).astype(bf16)
            queries = jnp.concatenate([ask, shared, ask, jnp.zeros_like(shared)], 0)
            logits.append(dot(queries, keys_ref[slot], (0, 0)))

    total = None
    pick = lax.broadcasted_iota(jnp.int32, (part, lanes), 0) == chans
    pick = jnp.where(pick, 1.0, 0.0).astype(bf16)
    for place, scores in enumerate(logits):
        slot, head = divmod(place, 2)
        peak = jnp.broadcast_to(jnp.max(scores, 1, keepdims=True), (rows, lanes))
        if before:
            old_peak = refs[6 + count][place]
            peak = jnp.maximum(peak, old_peak)
        expo = jnp.exp2(scores - jnp.concatenate([peak] * (size // lanes), 1)).astype(bf16)
        mixed = dot(expo, keys_ref[slot], (1, 1))
        if before:
            factor = jnp.exp2(old_peak - peak)
            factor = jnp.concatenate([factor, factor[:, : 2 * part - lanes]], 1)
            mixed += refs[5 + count][place] * factor
        if last:
            main = jnp.concatenate([jnp.concatenate([mains[slot][head], pick], 1)] * 2, 0)
            term = dot(mixed.astype(bf16), main)
            term = term[:, :lanes] * (terms[slot][1] / term[:, lanes:])
            total = term if total is None else total + term
        else:
            refs[-3][place] = mixed
            refs[-2][place] = peak
    if last:
        refs[-2][...] = total.T[chans:].astype(bf16)


def attend(terms, packs, own, tokens, state=(), last=True):
    rows = own.shape[1]
    count = len(tokens)
    pairs = 2 * count * rows * rows * len(terms)
    shape = [
        jax.ShapeDtypeStruct((2 * len(terms), rows, 2 * part), f32),
        jax.ShapeDtypeStruct((2 * len(terms), rows, lanes), f32),
    ]
    if last:
        shape = jax.ShapeDtypeStruct(own.shape, bf16)
    return pl.pallas_call(
        functools.partial(attend_kernel, terms, count, bool(state), last),
        in_specs=[pl.BlockSpec(memory_space=pltpu.VMEM)] * (5 + count + len(state)),
        out_specs=jax.tree.map(lambda _: pl.BlockSpec(memory_space=pltpu.VMEM), shape),
        out_shape=shape,
        scratch_shapes=[pltpu.VMEM((len(terms), 2 * part, count * rows), bf16)],
        compiler_params=pltpu.CompilerParams(vmem_limit_bytes=48 * 1024 * 1024),
        cost_estimate=pl.CostEstimate(
            flops=16 * pairs * lanes, bytes_accessed=1_000_000, transcendentals=pairs
        ),
        name="attend",
    )(*packs, own, *tokens, *state)


def swap(value, axis, flip, cross=0):
    axes = (axis, "tp")
    flip = 2 * flip + cross
    return lax.ppermute(value, axes, [(i, i ^ flip) for i in range(lax.axis_size(axes))])


def swap_all(value, axis, cross):
    one, three, two = (
        swap(value, axis, flip, crossed)
        for flip, crossed in ((1, cross[0]), (3, cross[2]), (2, cross[1]))
    )
    return [value, one, two, three]


def other_core(value):
    return lax.ppermute(value, "tp", [(0, 1), (1, 0)])


def add_over(value, axis):
    sent = lax.optimization_barrier(value.astype(bf16))
    parts = [part.astype(f32) for part in swap_all(sent, axis, (1, 0, 1))]
    return (parts[0] + parts[1]) + (parts[2] + parts[3])


def add_heads(value):
    return add_over(add_over(value, "y"), "x")


def shards(
    latent_noise, score_noise, gen_step, score_step, embed_weight, qkv_weight, mod_weight, head_out
):
    model = lax.axis_index("mp")
    gen_sigma = gen_step[0].astype(f32) / step_scale
    score_sigma = score_step[0].astype(f32) / step_scale
    latents, noise = latent_noise.T, score_noise.T
    odd = (lax.axis_index("x") + lax.axis_index("y")) % 2 == 1

    first = swap(latents, "mp", 1, 1)
    noise = jnp.where(odd, other_core(noise), noise)
    pack = fold_maps(
        gen_step, score_step, head_out[0, 0].T, embed_weight[0], mod_weight[0], qkv_weight[0, 0]
    )
    pack, first, noise = lax.optimization_barrier((pack, first, noise))
    other = swap(pack[:part], "zh", 1, 1)
    pair = swap(jnp.stack([latents, first]), "mp", 2, 1)
    packs = swap_all(jnp.concatenate([pack, other], 0), "mp", (1, 1, 1))
    near = [latents, first, pair[0], pair[1]]
    far = other_core(jnp.stack(near))

    latents = jnp.where(odd, far[0], latents)
    speed = add_heads(attend(((0, 1.0),), packs, latents, near + list(far)))
    clean = latents.astype(f32) - gen_sigma * speed
    noisy = (1.0 - score_sigma) * clean + score_sigma * noise.astype(f32)
    near = swap_all(noisy.astype(bf16), "mp", (1, 1, 1))
    far = other_core(jnp.stack(near))
    terms = ((1, 1.0), (2, -2.0), (3, 1.0))
    state = attend(terms, packs, near[0], near, last=False)
    grad = attend(terms, packs, near[0], list(far), state)
    grad = add_heads(grad) * -score_sigma
    grad = jnp.where(odd, other_core(grad), grad)
    clean = clean.astype(bf16)
    clean = jnp.where(odd, other_core(clean), clean)
    return (clean.T, grad.T)


def solution(mesh):
    models, heads, cores = mesh.devices.shape
    fine = Mesh(mesh.devices.reshape(models, 4, heads // 16, 4, cores), ("mp", "x", "zh", "y", "tp"))
    placed = (
        P(("mp", "tp"), None),
        P(("mp", "tp"), None),
        P(),
        P(),
        P("mp", None, None),
        P("mp", ("x", "zh", "y"), None, None),
        P("mp", None, None),
        P("mp", ("x", "zh", "y"), None, None),
    )
    return jax.shard_map(
        shards,
        mesh=fine,
        in_specs=placed,
        out_specs=(P(("mp", "tp"), None), P(("mp", "tp"), None)),
        check_vma=False,
    )
```

```python
import functools
import math

import jax
import jax.numpy as jnp
from jax import lax
from jax.experimental import pallas as pl
from jax.experimental.pallas import tpu as pltpu
from jax.sharding import Mesh
from jax.sharding import PartitionSpec as P

norm_eps = 1e-06
step_scale = 1000.0
f32 = jnp.float32
bf16 = jnp.bfloat16
chunk = 1024
lanes = 128
part = 80


def frequencies(freq_count):
    half_freq = freq_count // 2
    index = lax.broadcasted_iota(jnp.int32, (1, half_freq), 1)
    total = jnp.ones((1, half_freq), f32)
    for bit in range(half_freq.bit_length() - 1):
        factor = 10000.0 ** (-2.0 * (1 << bit) / freq_count)
        total = total * jnp.where((index >> bit) & 1 == 1, factor, 1.0)
    return total


def cos_sin(angle):
    turn = jnp.floor(angle * (2.0 / math.pi) + 0.5)
    left = angle - turn * 1.5703125
    left = left - turn * 4.837512969970703125e-4
    left = left - turn * 7.54978995489188216e-8
    square = left * left
    sine = left + left * square * (
        -1.6666654611e-1 + square * (8.3321608736e-3 - square * 1.9515295891e-4)
    )
    cosine = (
        1.0
        - 0.5 * square
        + square
        * square
        * (4.166664568298827e-2 + square * (-1.388731625493765e-3 + square * 2.443315711809948e-5))
    )
    quarter = turn.astype(jnp.int32) & 3
    odd = (quarter & 1) == 1
    cos_out = jnp.where(odd, sine, cosine)
    sin_out = jnp.where(odd, cosine, sine)
    cos_out = jnp.where((quarter == 1) | (quarter == 2), -cos_out, cos_out)
    sin_out = jnp.where(quarter >= 2, -sin_out, sin_out)
    return cos_out, sin_out


def dot(a, b, dims=(1, 0), precision=None):
    return lax.dot_general(
        a, b, (((dims[0],), (dims[1],)), ((), ())), precision=precision, preferred_element_type=f32
    )


def halves(value):
    high = value.astype(bf16)
    return high, (value - high.astype(f32)).astype(bf16)


def dot_halves(a, b):
    a_high, a_low = halves(a)
    b_high, b_low = halves(b)
    return dot(
        jnp.concatenate([a_high, a_high, a_low], 0),
        jnp.concatenate([b_high, b_low, b_high], 0),
        (0, 0),
    )


def maps_kernel(
    gen_ref, score_ref, embed_hbm, head_hbm, mod_hbm, weight_hbm, out_ref,
    embed_ref, head_ref, mod_ref, weight_ref, sems,
):
    chans, head_size = head_ref.shape
    width = embed_ref.shape[1]
    steps = width // chunk
    small = [
        pltpu.make_async_copy(source, target, sems.at[at])
        for at, (source, target) in enumerate(
            ((embed_hbm, embed_ref), (head_hbm, head_ref))
        )
    ]
    for copy in small:
        copy.start()
    copies = []
    for step in range(steps):
        mine = []
        for kind, (source, target, offset) in enumerate(
            ((mod_hbm, mod_ref, 0), (mod_hbm, mod_ref, width), (weight_hbm, weight_ref, 0))
        ):
            at = pl.ds(offset + step * chunk, chunk)
            copy = pltpu.make_async_copy(
                source.at[:, at], target.at[:, at], sems.at[2 + 3 * step + kind]
            )
            copy.start()
            mine.append(copy)
        copies.append(mine)

    small[0].wait()
    mean = jnp.sum(embed_ref[...].astype(f32), 1, keepdims=True) * (1.0 / width)
    ones = jnp.ones((part - chans, chunk), bf16)
    row_at = lax.broadcasted_iota(jnp.int32, (lanes - chans, chunk), 0)
    own_step = jnp.where(lax.axis_index("mp") == 0, gen_ref[0], score_ref[0]).astype(f32)
    waves = cos_sin(frequencies(2 * lanes) * own_step)
    freq = jnp.concatenate([jnp.broadcast_to(wave, (lanes, lanes)).T for wave in waves], 0)
    maps = gram = None
    for step in range(steps):
        own = embed_ref[:, pl.ds(step * chunk, chunk)]
        gram_term = dot(jnp.concatenate([own, ones], 0), own, (1, 1))
        rows = []
        copies[step][0].wait()
        copies[step][1].wait()
        for kind in range(2):
            total = None
            for at in range(0, freq.shape[0], 16):
                here = mod_ref[at : at + 16, pl.ds(kind * width + step * chunk, chunk)]
                scale = jnp.concatenate([freq[at : at + 16]] * (chunk // lanes), 1)
                term = here.astype(f32) * scale
                total = term if total is None else total + term
            rows.append(jnp.sum(total, 0, keepdims=True))
        centred = (own.astype(f32) - mean) * (1.0 + rows[1])
        tail = jnp.where(row_at == 0, jnp.broadcast_to(rows[0], row_at.shape), 0.0)
        lifted = jnp.concatenate([centred.astype(bf16), tail.astype(bf16)], 0)
        copies[step][2].wait()
        maps_term = dot(weight_ref[:, pl.ds(step * chunk, chunk)], lifted, (1, 1))
        maps = maps_term if maps is None else maps + maps_term
        gram = gram_term if gram is None else gram + gram_term

    map_q = maps[:head_size] * (head_size ** (-0.5) * math.log2(math.e))
    map_k = maps[head_size : 2 * head_size]
    map_v = maps[2 * head_size :]
    lane = lax.broadcasted_iota(jnp.int32, (head_size, lanes), 1)
    small[1].wait()
    wide_head = jnp.concatenate([jnp.zeros_like(head_ref), head_ref[...]], 0)
    main = dot_halves(map_q, jnp.where(lane < chans, map_k, 0.0))
    high, low = halves(map_v)
    main += dot(high, wide_head, (0, 1)) + dot(low, wide_head, (0, 1))
    last = dot_halves(map_k, map_q)[chans : chans + 1]
    main = main[:part]
    row = lax.broadcasted_iota(jnp.int32, main.shape, 0)
    main = jnp.where(row == chans + 1, jnp.broadcast_to(last, main.shape), main)
    out_ref[:part] = main.astype(bf16)
    gram = gram * (1.0 / width)
    high, low = halves(gram[:chans] - mean * gram[chans : chans + 1])
    out_ref[part:] = jnp.concatenate([high.astype(f32), low.astype(f32)], 1).astype(bf16)


def fold_maps(gen_step, score_step, head, embed, mod_weight, weight):
    chans, width = embed.shape
    return pl.pallas_call(
        maps_kernel,
        in_specs=[pl.BlockSpec(memory_space=pltpu.SMEM)] * 2
        + [pl.BlockSpec(memory_space=pl.ANY)] * 4,
        out_specs=pl.BlockSpec(memory_space=pltpu.VMEM),
        out_shape=jax.ShapeDtypeStruct((part + chans, lanes), bf16),
        scratch_shapes=[
            pltpu.VMEM(embed.shape, bf16),
            pltpu.VMEM(head.shape, bf16),
            pltpu.VMEM(mod_weight.shape, bf16),
            pltpu.VMEM(weight.shape, bf16),
            pltpu.SemaphoreType.DMA((2 + 3 * (width // chunk),)),
        ],
        compiler_params=pltpu.CompilerParams(vmem_limit_bytes=56_000_000),
        cost_estimate=pl.CostEstimate(
            flops=6_000_000_000, bytes_accessed=10_000_000, transcendentals=0
        ),
        name="fold_maps",
    )(gen_step, score_step, embed, head, mod_weight, weight)


def attend_kernel(terms, count, before, last, *refs):
    refs = list(refs)
    pack_refs, own_ref, token_refs = refs[:4], refs[4], refs[5 : 5 + count]
    keys_ref = refs[-1]
    chans, rows = own_ref.shape
    size = count * rows
    here, upper = lax.axis_index("mp"), lax.axis_index("zh") == 1

    mains, spreads = [], []
    for model, _ in terms:
        at = here ^ model
        pack = pack_refs[0][...]
        for other in range(1, 4):
            pack = jnp.where(at == other, pack_refs[other][...], pack)
        one, two = pack[:part], pack[part + chans :]
        mains.append((jnp.where(upper, two, one), jnp.where(upper, one, two)))
        spreads.append(pack[part : part + chans])

    tokens = jnp.concatenate([ref[...] for ref in token_refs] + [own_ref[...]], 1)
    wide = tokens.astype(f32)
    spread = dot(jnp.concatenate(spreads, 0), jnp.concatenate([tokens, tokens], 0))
    row = lax.broadcasted_iota(jnp.int32, (part - chans, size + rows), 0)
    one = jnp.where(row == 0, 1.0, 0.0).astype(bf16)
    logits = []
    for slot, heads in enumerate(mains):
        product = spread[slot * chans : (slot + 1) * chans] * wide
        variance = jnp.maximum(jnp.sum(product, 0, keepdims=True), 0.0)
        normed = wide * lax.rsqrt(variance + norm_eps)
        high = normed.astype(bf16)
        low = (normed - high.astype(f32)).astype(bf16)
        features = jnp.concatenate([high, one, low, jnp.zeros_like(one)], 0)
        keys_ref[slot] = features[:, :size]
        own = features[:, size:]
        own_high = jnp.concatenate([own[:part], jnp.zeros((lanes - part, rows), bf16)], 0)
        for main in heads:
            ask = dot(jnp.concatenate([main, main], 0), own, (0, 0))[:chans].astype(bf16)
            shared = jnp.broadcast_to(dot(main[chans:], own_high)[1:2], (part - chans, rows))
            shared = jnp.where(row[:, :rows] == 0, shared, 0.0).astype(bf16)
            queries = jnp.concatenate([ask, shared, ask, jnp.zeros_like(shared)], 0)
            logits.append(dot(queries, keys_ref[slot], (0, 0)))

    total = None
    pick = lax.broadcasted_iota(jnp.int32, (part, lanes), 0) == chans
    pick = jnp.where(pick, 1.0, 0.0).astype(bf16)
    for place, scores in enumerate(logits):
        slot, head = divmod(place, 2)
        peak = jnp.broadcast_to(jnp.max(scores, 1, keepdims=True), (rows, lanes))
        if before:
            old_peak = refs[6 + count][place]
            peak = jnp.maximum(peak, old_peak)
        expo = jnp.exp2(scores - jnp.concatenate([peak] * (size // lanes), 1)).astype(bf16)
        mixed = dot(expo, keys_ref[slot], (1, 1))
        if before:
            factor = jnp.exp2(old_peak - peak)
            factor = jnp.concatenate([factor, factor[:, : 2 * part - lanes]], 1)
            mixed += refs[5 + count][place] * factor
        if last:
            main = jnp.concatenate([jnp.concatenate([mains[slot][head], pick], 1)] * 2, 0)
            term = dot(mixed.astype(bf16), main)
            term = term[:, :lanes] * (terms[slot][1] / term[:, lanes:])
            total = term if total is None else total + term
        else:
            refs[-3][place] = mixed
            refs[-2][place] = peak
    if last:
        refs[-2][...] = total.T[chans:].astype(bf16)


def attend(terms, packs, own, tokens, state=(), last=True):
    rows = own.shape[1]
    count = len(tokens)
    pairs = 2 * count * rows * rows * len(terms)
    shape = [
        jax.ShapeDtypeStruct((2 * len(terms), rows, 2 * part), f32),
        jax.ShapeDtypeStruct((2 * len(terms), rows, lanes), f32),
    ]
    if last:
        shape = jax.ShapeDtypeStruct(own.shape, bf16)
    return pl.pallas_call(
        functools.partial(attend_kernel, terms, count, bool(state), last),
        in_specs=[pl.BlockSpec(memory_space=pltpu.VMEM)] * (5 + count + len(state)),
        out_specs=jax.tree.map(lambda _: pl.BlockSpec(memory_space=pltpu.VMEM), shape),
        out_shape=shape,
        scratch_shapes=[pltpu.VMEM((len(terms), 2 * part, count * rows), bf16)],
        compiler_params=pltpu.CompilerParams(vmem_limit_bytes=48 * 1024 * 1024),
        cost_estimate=pl.CostEstimate(
            flops=16 * pairs * lanes, bytes_accessed=1_000_000, transcendentals=pairs
        ),
        name="attend",
    )(*packs, own, *tokens, *state)


def swap(value, axis, flip, cross=0):
    axes = (axis, "tp")
    flip = 2 * flip + cross
    return lax.ppermute(value, axes, [(i, i ^ flip) for i in range(lax.axis_size(axes))])


def swap_all(value, axis, cross):
    one, three, two = (
        swap(value, axis, flip, crossed)
        for flip, crossed in ((1, cross[0]), (3, cross[2]), (2, cross[1]))
    )
    return [value, one, two, three]


def other_core(value):
    return lax.ppermute(value, "tp", [(0, 1), (1, 0)])


def add_over(value, axis):
    sent = lax.optimization_barrier(value.astype(bf16))
    parts = [part.astype(f32) for part in swap_all(sent, axis, (0, 1, 1))]
    return (parts[0] + parts[1]) + (parts[2] + parts[3])


def add_heads(value):
    return add_over(add_over(value, "y"), "x")


def shards(
    latent_noise, score_noise, gen_step, score_step, embed_weight, qkv_weight, mod_weight, head_out
):
    model = lax.axis_index("mp")
    gen_sigma = gen_step[0].astype(f32) / step_scale
    score_sigma = score_step[0].astype(f32) / step_scale
    latents, noise = latent_noise.T, score_noise.T
    odd = (lax.axis_index("x") // 2 + lax.axis_index("y") // 2) % 2 == 1

    first = swap(latents, "mp", 1, 1)
    noise = jnp.where(odd, other_core(noise), noise)
    pack = fold_maps(
        gen_step, score_step, head_out[0, 0].T, embed_weight[0], mod_weight[0], qkv_weight[0, 0]
    )
    pack, first, noise = lax.optimization_barrier((pack, first, noise))
    other = swap(pack[:part], "zh", 1, 1)
    pair = swap(jnp.stack([latents, first]), "mp", 2, 1)
    packs = swap_all(jnp.concatenate([pack, other], 0), "mp", (1, 1, 1))
    near = [latents, first, pair[0], pair[1]]
    far = other_core(jnp.stack(near))

    latents = jnp.where(odd, far[0], latents)
    speed = add_heads(attend(((0, 1.0),), packs, latents, near + list(far)))
    clean = latents.astype(f32) - gen_sigma * speed
    noisy = (1.0 - score_sigma) * clean + score_sigma * noise.astype(f32)
    near = swap_all(noisy.astype(bf16), "mp", (1, 1, 1))
    far = other_core(jnp.stack(near))
    terms = ((1, 1.0), (2, -2.0), (3, 1.0))
    state = attend(terms, packs, near[0], near, last=False)
    grad = attend(terms, packs, near[0], list(far), state)
    grad = add_heads(grad) * -score_sigma
    grad = jnp.where(odd, other_core(grad), grad)
    clean = clean.astype(bf16)
    clean = jnp.where(odd, other_core(clean), clean)
    return (clean.T, grad.T)


def solution(mesh):
    models, heads, cores = mesh.devices.shape
    fine = Mesh(mesh.devices.reshape(models, 4, heads // 16, 4, cores), ("mp", "x", "zh", "y", "tp"))
    placed = (
        P(("mp", "tp"), None),
        P(("mp", "tp"), None),
        P(),
        P(),
        P("mp", None, None),
        P("mp", ("x", "zh", "y"), None, None),
        P("mp", None, None),
        P("mp", ("x", "zh", "y"), None, None),
    )
    return jax.shard_map(
        shards,
        mesh=fine,
        in_specs=placed,
        out_specs=(P(("mp", "tp"), None), P(("mp", "tp"), None)),
        check_vma=False,
    )
```

```python
import functools
import math

import jax
import jax.numpy as jnp
from jax import lax
from jax.experimental import pallas as pl
from jax.experimental.pallas import tpu as pltpu
from jax.sharding import Mesh
from jax.sharding import PartitionSpec as P

norm_eps = 1e-06
step_scale = 1000.0
f32 = jnp.float32
bf16 = jnp.bfloat16
chunk = 1024
lanes = 128
part = 80


def frequencies(freq_count):
    half_freq = freq_count // 2
    index = lax.broadcasted_iota(jnp.int32, (1, half_freq), 1)
    total = jnp.ones((1, half_freq), f32)
    for bit in range(half_freq.bit_length() - 1):
        factor = 10000.0 ** (-2.0 * (1 << bit) / freq_count)
        total = total * jnp.where((index >> bit) & 1 == 1, factor, 1.0)
    return total


def cos_sin(angle):
    turn = jnp.floor(angle * (2.0 / math.pi) + 0.5)
    left = angle - turn * 1.5703125
    left = left - turn * 4.837512969970703125e-4
    left = left - turn * 7.54978995489188216e-8
    square = left * left
    sine = left + left * square * (
        -1.6666654611e-1 + square * (8.3321608736e-3 - square * 1.9515295891e-4)
    )
    cosine = (
        1.0
        - 0.5 * square
        + square
        * square
        * (4.166664568298827e-2 + square * (-1.388731625493765e-3 + square * 2.443315711809948e-5))
    )
    quarter = turn.astype(jnp.int32) & 3
    odd = (quarter & 1) == 1
    cos_out = jnp.where(odd, sine, cosine)
    sin_out = jnp.where(odd, cosine, sine)
    cos_out = jnp.where((quarter == 1) | (quarter == 2), -cos_out, cos_out)
    sin_out = jnp.where(quarter >= 2, -sin_out, sin_out)
    return cos_out, sin_out


def dot(a, b, dims=(1, 0), precision=None):
    return lax.dot_general(
        a, b, (((dims[0],), (dims[1],)), ((), ())), precision=precision, preferred_element_type=f32
    )


def halves(value):
    high = value.astype(bf16)
    return high, (value - high.astype(f32)).astype(bf16)


def dot_halves(a, b):
    a_high, a_low = halves(a)
    b_high, b_low = halves(b)
    return dot(
        jnp.concatenate([a_high, a_high, a_low], 0),
        jnp.concatenate([b_high, b_low, b_high], 0),
        (0, 0),
    )


def maps_kernel(
    gen_ref, score_ref, embed_hbm, head_hbm, mod_hbm, weight_hbm, out_ref,
    embed_ref, head_ref, mod_ref, weight_ref, sems,
):
    chans, head_size = head_ref.shape
    width = embed_ref.shape[1]
    steps = width // chunk
    small = [
        pltpu.make_async_copy(source, target, sems.at[at])
        for at, (source, target) in enumerate(
            ((embed_hbm, embed_ref), (head_hbm, head_ref))
        )
    ]
    for copy in small:
        copy.start()
    copies = []
    for step in range(steps):
        mine = []
        for kind, (source, target, offset) in enumerate(
            ((mod_hbm, mod_ref, 0), (mod_hbm, mod_ref, width), (weight_hbm, weight_ref, 0))
        ):
            at = pl.ds(offset + step * chunk, chunk)
            copy = pltpu.make_async_copy(
                source.at[:, at], target.at[:, at], sems.at[2 + 3 * step + kind]
            )
            copy.start()
            mine.append(copy)
        copies.append(mine)

    small[0].wait()
    mean = jnp.sum(embed_ref[...].astype(f32), 1, keepdims=True) * (1.0 / width)
    ones = jnp.ones((part - chans, chunk), bf16)
    row_at = lax.broadcasted_iota(jnp.int32, (lanes - chans, chunk), 0)
    own_step = jnp.where(lax.axis_index("mp") == 0, gen_ref[0], score_ref[0]).astype(f32)
    waves = cos_sin(frequencies(2 * lanes) * own_step)
    freq = jnp.concatenate([jnp.broadcast_to(wave, (lanes, lanes)).T for wave in waves], 0)
    maps = gram = None
    for step in range(steps):
        own = embed_ref[:, pl.ds(step * chunk, chunk)]
        gram_term = dot(jnp.concatenate([own, ones], 0), own, (1, 1))
        rows = []
        copies[step][0].wait()
        copies[step][1].wait()
        for kind in range(2):
            total = None
            for at in range(0, freq.shape[0], 16):
                here = mod_ref[at : at + 16, pl.ds(kind * width + step * chunk, chunk)]
                scale = jnp.concatenate([freq[at : at + 16]] * (chunk // lanes), 1)
                term = here.astype(f32) * scale
                total = term if total is None else total + term
            rows.append(jnp.sum(total, 0, keepdims=True))
        centred = (own.astype(f32) - mean) * (1.0 + rows[1])
        tail = jnp.where(row_at == 0, jnp.broadcast_to(rows[0], row_at.shape), 0.0)
        lifted = jnp.concatenate([centred.astype(bf16), tail.astype(bf16)], 0)
        copies[step][2].wait()
        maps_term = dot(weight_ref[:, pl.ds(step * chunk, chunk)], lifted, (1, 1))
        maps = maps_term if maps is None else maps + maps_term
        gram = gram_term if gram is None else gram + gram_term

    map_q = maps[:head_size] * (head_size ** (-0.5) * math.log2(math.e))
    map_k = maps[head_size : 2 * head_size]
    map_v = maps[2 * head_size :]
    lane = lax.broadcasted_iota(jnp.int32, (head_size, lanes), 1)
    small[1].wait()
    wide_head = jnp.concatenate([jnp.zeros_like(head_ref), head_ref[...]], 0)
    main = dot_halves(map_q, jnp.where(lane < chans, map_k, 0.0))
    high, low = halves(map_v)
    main += dot(high, wide_head, (0, 1)) + dot(low, wide_head, (0, 1))
    last = dot_halves(map_k, map_q)[chans : chans + 1]
    main = main[:part]
    row = lax.broadcasted_iota(jnp.int32, main.shape, 0)
    main = jnp.where(row == chans + 1, jnp.broadcast_to(last, main.shape), main)
    out_ref[:part] = main.astype(bf16)
    gram = gram * (1.0 / width)
    high, low = halves(gram[:chans] - mean * gram[chans : chans + 1])
    out_ref[part:] = jnp.concatenate([high.astype(f32), low.astype(f32)], 1).astype(bf16)


def fold_maps(gen_step, score_step, head, embed, mod_weight, weight):
    chans, width = embed.shape
    return pl.pallas_call(
        maps_kernel,
        in_specs=[pl.BlockSpec(memory_space=pltpu.SMEM)] * 2
        + [pl.BlockSpec(memory_space=pl.ANY)] * 4,
        out_specs=pl.BlockSpec(memory_space=pltpu.VMEM),
        out_shape=jax.ShapeDtypeStruct((part + chans, lanes), bf16),
        scratch_shapes=[
            pltpu.VMEM(embed.shape, bf16),
            pltpu.VMEM(head.shape, bf16),
            pltpu.VMEM(mod_weight.shape, bf16),
            pltpu.VMEM(weight.shape, bf16),
            pltpu.SemaphoreType.DMA((2 + 3 * (width // chunk),)),
        ],
        compiler_params=pltpu.CompilerParams(vmem_limit_bytes=56_000_000),
        cost_estimate=pl.CostEstimate(
            flops=6_000_000_000, bytes_accessed=10_000_000, transcendentals=0
        ),
        name="fold_maps",
    )(gen_step, score_step, embed, head, mod_weight, weight)


def attend_kernel(terms, count, before, last, *refs):
    refs = list(refs)
    pack_refs, own_ref, token_refs = refs[:4], refs[4], refs[5 : 5 + count]
    keys_ref = refs[-1]
    chans, rows = own_ref.shape
    size = count * rows
    here, upper = lax.axis_index("mp"), lax.axis_index("zh") == 1

    mains, spreads = [], []
    for model, _ in terms:
        at = here ^ model
        pack = pack_refs[0][...]
        for other in range(1, 4):
            pack = jnp.where(at == other, pack_refs[other][...], pack)
        one, two = pack[:part], pack[part + chans :]
        mains.append((jnp.where(upper, two, one), jnp.where(upper, one, two)))
        spreads.append(pack[part : part + chans])

    tokens = jnp.concatenate([ref[...] for ref in token_refs] + [own_ref[...]], 1)
    wide = tokens.astype(f32)
    spread = dot(jnp.concatenate(spreads, 0), jnp.concatenate([tokens, tokens], 0))
    row = lax.broadcasted_iota(jnp.int32, (part - chans, size + rows), 0)
    one = jnp.where(row == 0, 1.0, 0.0).astype(bf16)
    logits = []
    for slot, heads in enumerate(mains):
        product = spread[slot * chans : (slot + 1) * chans] * wide
        variance = jnp.maximum(jnp.sum(product, 0, keepdims=True), 0.0)
        normed = wide * lax.rsqrt(variance + norm_eps)
        high = normed.astype(bf16)
        low = (normed - high.astype(f32)).astype(bf16)
        features = jnp.concatenate([high, one, low, jnp.zeros_like(one)], 0)
        keys_ref[slot] = features[:, :size]
        own = features[:, size:]
        own_high = jnp.concatenate([own[:part], jnp.zeros((lanes - part, rows), bf16)], 0)
        for main in heads:
            ask = dot(jnp.concatenate([main, main], 0), own, (0, 0))[:chans].astype(bf16)
            shared = jnp.broadcast_to(dot(main[chans:], own_high)[1:2], (part - chans, rows))
            shared = jnp.where(row[:, :rows] == 0, shared, 0.0).astype(bf16)
            queries = jnp.concatenate([ask, shared, ask, jnp.zeros_like(shared)], 0)
            logits.append(dot(queries, keys_ref[slot], (0, 0)))

    total = None
    pick = lax.broadcasted_iota(jnp.int32, (part, lanes), 0) == chans
    pick = jnp.where(pick, 1.0, 0.0).astype(bf16)
    for place, scores in enumerate(logits):
        slot, head = divmod(place, 2)
        peak = jnp.broadcast_to(jnp.max(scores, 1, keepdims=True), (rows, lanes))
        if before:
            old_peak = refs[6 + count][place]
            peak = jnp.maximum(peak, old_peak)
        expo = jnp.exp2(scores - jnp.concatenate([peak] * (size // lanes), 1)).astype(bf16)
        mixed = dot(expo, keys_ref[slot], (1, 1))
        if before:
            factor = jnp.exp2(old_peak - peak)
            factor = jnp.concatenate([factor, factor[:, : 2 * part - lanes]], 1)
            mixed += refs[5 + count][place] * factor
        if last:
            main = jnp.concatenate([jnp.concatenate([mains[slot][head], pick], 1)] * 2, 0)
            term = dot(mixed.astype(bf16), main)
            term = term[:, :lanes] * (terms[slot][1] / term[:, lanes:])
            total = term if total is None else total + term
        else:
            refs[-3][place] = mixed
            refs[-2][place] = peak
    if last:
        refs[-2][...] = total.T[chans:].astype(bf16)


def attend(terms, packs, own, tokens, state=(), last=True):
    rows = own.shape[1]
    count = len(tokens)
    pairs = 2 * count * rows * rows * len(terms)
    shape = [
        jax.ShapeDtypeStruct((2 * len(terms), rows, 2 * part), f32),
        jax.ShapeDtypeStruct((2 * len(terms), rows, lanes), f32),
    ]
    if last:
        shape = jax.ShapeDtypeStruct(own.shape, bf16)
    return pl.pallas_call(
        functools.partial(attend_kernel, terms, count, bool(state), last),
        in_specs=[pl.BlockSpec(memory_space=pltpu.VMEM)] * (5 + count + len(state)),
        out_specs=jax.tree.map(lambda _: pl.BlockSpec(memory_space=pltpu.VMEM), shape),
        out_shape=shape,
        scratch_shapes=[pltpu.VMEM((len(terms), 2 * part, count * rows), bf16)],
        compiler_params=pltpu.CompilerParams(vmem_limit_bytes=48 * 1024 * 1024),
        cost_estimate=pl.CostEstimate(
            flops=16 * pairs * lanes, bytes_accessed=1_000_000, transcendentals=pairs
        ),
        name="attend",
    )(*packs, own, *tokens, *state)


def swap(value, axis, flip, cross=0):
    axes = (axis, "tp")
    flip = 2 * flip + cross
    return lax.ppermute(value, axes, [(i, i ^ flip) for i in range(lax.axis_size(axes))])


def swap_all(value, axis, cross):
    one, three, two = (
        swap(value, axis, flip, crossed)
        for flip, crossed in ((1, cross[0]), (3, cross[2]), (2, cross[1]))
    )
    return [value, one, two, three]


def other_core(value):
    return lax.ppermute(value, "tp", [(0, 1), (1, 0)])


def add_over(value, axis):
    sent = lax.optimization_barrier(value.astype(bf16))
    parts = [part.astype(f32) for part in swap_all(sent, axis, (1, 0, 1))]
    return (parts[0] + parts[1]) + (parts[2] + parts[3])


def add_heads(value):
    return add_over(add_over(value, "y"), "x")


def shards(
    latent_noise, score_noise, gen_step, score_step, embed_weight, qkv_weight, mod_weight, head_out
):
    model = lax.axis_index("mp")
    gen_sigma = gen_step[0].astype(f32) / step_scale
    score_sigma = score_step[0].astype(f32) / step_scale
    latents, noise = latent_noise.T, score_noise.T
    odd = (lax.axis_index("x") + lax.axis_index("y")) % 2 == 1

    first = swap(latents, "mp", 1, 1)
    noise = jnp.where(odd, other_core(noise), noise)
    pack = fold_maps(
        gen_step, score_step, head_out[0, 0].T, embed_weight[0], mod_weight[0], qkv_weight[0, 0]
    )
    pack, first, noise = lax.optimization_barrier((pack, first, noise))
    other = swap(pack[:part], "zh", 1, 1)
    pair = swap(jnp.stack([latents, first]), "mp", 2, 1)
    packs = swap_all(jnp.concatenate([pack, other], 0), "mp", (1, 1, 1))
    near = [latents, first, pair[0], pair[1]]
    far = other_core(jnp.stack(near))

    latents = jnp.where(odd, far[0], latents)
    speed = add_heads(attend(((0, 1.0),), packs, latents, near + list(far)))
    clean = latents.astype(f32) - gen_sigma * speed
    noisy = (1.0 - score_sigma) * clean + score_sigma * noise.astype(f32)
    near = swap_all(noisy.astype(bf16), "mp", (1, 1, 1))
    far = other_core(jnp.stack(near))
    terms = ((1, 1.0), (2, -2.0), (3, 1.0))
    grad = attend(terms, packs, near[0], near + list(far))
    grad = add_heads(grad) * -score_sigma
    grad = jnp.where(odd, other_core(grad), grad)
    clean = clean.astype(bf16)
    clean = jnp.where(odd, other_core(clean), clean)
    return (clean.T, grad.T)


def solution(mesh):
    models, heads, cores = mesh.devices.shape
    fine = Mesh(mesh.devices.reshape(models, 4, heads // 16, 4, cores), ("mp", "x", "zh", "y", "tp"))
    placed = (
        P(("mp", "tp"), None),
        P(("mp", "tp"), None),
        P(),
        P(),
        P("mp", None, None),
        P("mp", ("x", "zh", "y"), None, None),
        P("mp", None, None),
        P("mp", ("x", "zh", "y"), None, None),
    )
    return jax.shard_map(
        shards,
        mesh=fine,
        in_specs=placed,
        out_specs=(P(("mp", "tp"), None), P(("mp", "tp"), None)),
        check_vma=False,
    )
```
